128 devices in a mesh: pipe: 16 (over z_hi, x, core), tensor: 8 (over y, z_lo).
Axes of the slice: x: 4, y: 4, z: 4 (z_hi: 2, z_lo: 2; z = z_hi * 2 + z_lo), core: 2. Of those that a mesh axis runs over, the one named last changes fastest.
Arguments:
- entry_symbol_ids: int32 [1024], replicated, may hold values from 0 to 131071
- lookup_table_matrix: bfloat16 [131072, 4096], P('pipe', 'tensor'), may hold values from -6 to 6
- pending_batches: bfloat16 [16384, 4096], P(('pipe', 'tensor')), may hold values from -6 to 6
- scale_factors: float32 [16, 4096], P('pipe'), may hold values from 0.25 to 1.75
- query_projector: bfloat16 [16, 4096, 4096], P('pipe', None, 'tensor'), may hold values from -0.0625 to 0.0625
- key_projector: bfloat16 [16, 4096, 512], P('pipe', None, 'tensor'), may hold values from -1.25 to 1.25
- value_projector: bfloat16 [16, 4096, 512], P('pipe', None, 'tensor'), may hold values from -0.09375 to 0.09375
- result_projector: bfloat16 [16, 4096, 4096], P('pipe', 'tensor'), may hold values from -0.75 to 0.75
Outputs:
- block_results: float32 [16384, 4096], P(('pipe', 'tensor'))
- second_out: float32 [16384, 4096], P(('pipe', 'tensor'))
The draws below stay inside these ranges and needn't reach their ends.
All inputs are finite; a program needn't handle non-finite values.
Results may differ from the reference program's by a relative error of at most 0.035.
The reference program's roundings to bfloat16 on the way (of `embedded`, `normed`, `attn_weights` and `context`) count: a program that leaves them out, or rounds other values in their place, can miss the bound.
Values may be sent and summed in bfloat16 or wider, within the bound.
A program may use at most 192 MiB of HBM per device.

```python
import jax
import jax.numpy as jnp
from jax import lax

FEATURE_SPAN = 4096
HEADS = 32
KV_HEADS = 4
HEAD_DIM = 128
BATCH_SYMBOLS = 1024
LINKED_PARTS = 16
VOCAB = 131072


def query_base(key):
    values = jax.random.truncated_normal(key, -4.0, 4.0, (LINKED_PARTS, FEATURE_SPAN, HEADS * HEAD_DIM), jnp.float32)
    return values * FEATURE_SPAN ** (-0.5)


def draw_query_projector(key, part):
    return query_base(key).astype(jnp.bfloat16)


def draw_key_projector(key, part):
    key = jax.random.fold_in(key, 5)
    own_part = jax.random.truncated_normal(jax.random.fold_in(key, 1), -4.0, 4.0, (LINKED_PARTS, FEATURE_SPAN, KV_HEADS, HEAD_DIM), jnp.float32) * FEATURE_SPAN ** (-0.5)
    return own_part.reshape(LINKED_PARTS, FEATURE_SPAN, KV_HEADS * HEAD_DIM).astype(jnp.bfloat16)


def touch_ends(drawn, key, smallest, top_value):
    longest = drawn.shape.index(max(drawn.shape))
    spots = []
    for shift in (0, 1):
        where = [jax.random.randint(jax.random.fold_in(key, axis), (), 0, length) for axis, length in enumerate(drawn.shape)]
        where[longest] = (where[longest] + shift) % drawn.shape[longest]
        spots.append(tuple(where))
    return drawn.at[spots[0]].set(smallest).at[spots[1]].set(top_value)


def block_levels(key, extent, cuts, least, top_value):
    factor_of, own = 1.0, jax.random.fold_in(key, 6)
    for dim, parts in cuts:
        steps = jnp.exp(jax.random.uniform(jax.random.fold_in(own, dim), (parts,), jnp.float32, least / len(cuts), top_value / len(cuts)))
        factor_of = factor_of * jnp.repeat(steps, extent[dim] // parts).reshape([-1 if axis == dim else 1 for axis in range(len(extent))])
    return factor_of


def bell_draw(own_key, dims, width, limit, pieces=(), held_as=jnp.bfloat16):
    drawn = width * jax.random.normal(own_key, dims, jnp.float32)
    if pieces:
        drawn = drawn * block_levels(own_key, dims, pieces, -0.22, 0.18)
    return jnp.clip(drawn, -limit, limit).astype(held_as)


def setup_inputs(seed: int = 0) -> dict:
    splits = jax.random.split(jax.random.key(seed), 9)
    entry_symbol_ids = touch_ends(jax.random.randint(splits[0], (BATCH_SYMBOLS,), 0, VOCAB), jax.random.fold_in(splits[0], 1), 0, VOCAB - 1).astype(jnp.int32)
    lookup_table_matrix = bell_draw(splits[1], (VOCAB, FEATURE_SPAN), 1.0, 6.0, ((0, 16), (1, 8)))
    pending_batches = bell_draw(splits[2], (LINKED_PARTS * BATCH_SYMBOLS, FEATURE_SPAN), 1.0, 6.0, ((0, 128),))
    scale_factors = jnp.clip(1.0 + 0.15 * jax.random.normal(splits[3], (LINKED_PARTS, FEATURE_SPAN), jnp.float32), 0.25, 1.75)
    query_projector = draw_query_projector(jax.random.fold_in(splits[8], 71), 0)
    key_projector = draw_key_projector(jax.random.fold_in(splits[8], 71), 0)
    value_projector = bell_draw(splits[6], (LINKED_PARTS, FEATURE_SPAN, KV_HEADS * HEAD_DIM), FEATURE_SPAN ** -0.5, 0.09375, ((0, 16), (2, 8)))
    result_projector = bell_draw(splits[7], (LINKED_PARTS, HEADS * HEAD_DIM, FEATURE_SPAN), (3.0 * (HEADS * HEAD_DIM) ** -0.5), 0.75, ((0, 16), (1, 8)))
    return dict(entry_symbol_ids=entry_symbol_ids, lookup_table_matrix=lookup_table_matrix, pending_batches=pending_batches, scale_factors=scale_factors, query_projector=query_projector, key_projector=key_projector, value_projector=value_projector, result_projector=result_projector)


def shared_key_mixer(x_rows, gain_row, query_w, key_w, value_w, out_w):
    x_float = x_rows.astype(jnp.float32)
    normed = (x_float * lax.rsqrt(lax.optimization_barrier(jnp.mean(x_float * x_float, axis=1, keepdims=True)) + 1e-05) * gain_row).astype(jnp.bfloat16)
    queries = jnp.dot(normed, query_w, preferred_element_type=jnp.float32).astype(jnp.bfloat16)
    keys_all = jnp.dot(normed, key_w, preferred_element_type=jnp.float32).astype(jnp.bfloat16)
    values_all = jnp.dot(normed, value_w, preferred_element_type=jnp.float32).astype(jnp.bfloat16)
    group_size = HEADS // KV_HEADS
    query_heads = queries.reshape(BATCH_SYMBOLS, HEADS, HEAD_DIM).transpose(1, 0, 2).astype(jnp.float32)
    key_heads = jnp.repeat(keys_all.reshape(BATCH_SYMBOLS, KV_HEADS, HEAD_DIM).transpose(1, 0, 2), group_size, axis=0).astype(jnp.float32)
    value_heads = jnp.repeat(values_all.reshape(BATCH_SYMBOLS, KV_HEADS, HEAD_DIM).transpose(1, 0, 2), group_size, axis=0).astype(jnp.float32)
    scores = jnp.einsum('hqd,hkd->hqk', query_heads, key_heads) * HEAD_DIM ** (-0.5)
    positions = jnp.arange(BATCH_SYMBOLS, dtype=jnp.int32)
    causal_mask = positions[:, None] >= positions[None, :]
    scores = jnp.where(causal_mask[None], scores, jnp.float32(-1e+30))
    top_score = lax.optimization_barrier(jnp.max(scores, axis=2, keepdims=True))
    exp_scores = jnp.exp(scores - top_score)
    attn_weights = (exp_scores / lax.optimization_barrier(jnp.sum(exp_scores, axis=2, keepdims=True))).astype(jnp.bfloat16)
    context = jnp.einsum('hqk,hkd->hqd', attn_weights.astype(jnp.float32), value_heads).astype(jnp.bfloat16)
    context = context.transpose(1, 0, 2).reshape(BATCH_SYMBOLS, HEADS * HEAD_DIM)
    summed = jnp.dot(context, out_w, preferred_element_type=jnp.float32)
    return x_float + summed

def reference(entry_symbol_ids, lookup_table_matrix, pending_batches, scale_factors, query_projector, key_projector, value_projector, result_projector):

    def evaluate_block_step(operands):
        return shared_key_mixer(*operands)
    block_results = lax.map(evaluate_block_step, (pending_batches.reshape(LINKED_PARTS, BATCH_SYMBOLS, FEATURE_SPAN), scale_factors, query_projector, key_projector, value_projector, result_projector))
    embedded = jnp.take(lookup_table_matrix, entry_symbol_ids, axis=0).astype(jnp.float32)
    second_in = jnp.concatenate([embedded[None], block_results[:-1]], axis=0)
    second_out = lax.map(evaluate_block_step, (second_in, scale_factors, query_projector, key_projector, value_projector, result_projector))
    return (block_results.reshape(LINKED_PARTS * BATCH_SYMBOLS, FEATURE_SPAN), second_out.reshape(LINKED_PARTS * BATCH_SYMBOLS, FEATURE_SPAN))
```

```python
import functools

import jax
import jax.numpy as jnp
from jax import lax
from jax.experimental import pallas as pl
from jax.experimental.pallas import tpu as pltpu
from jax.sharding import PartitionSpec as P

HEAD_DIM = 128
MESH = pl.DeviceIdType.MESH
BOTH = ("pipe", "tensor")
RING = 4
TOKENS = 1024
ROWS = 128
WIDTH = 4096
HEADS_DEV = 4
PAIR = 2 * ROWS
HALF = ROWS // 2


def flat(pipe, tensor):
    return pipe * 8 + tensor


def physical(section, block):
    return flat(2 * (section // 2) + block % 2, 2 * (block // 2) + section % 2)


def traded(array):
    route = [(flat(s, t), physical(s, t)) for s in range(16) for t in range(8)]
    return lax.ppermute(array, BOTH, route)


def to_next_section(array):
    route = [(physical(s, t), physical(s + 1, t)) for s in range(15) for t in range(8)]
    return lax.ppermute(array, BOTH, route)


def layer_kernel(
    x_ref, gain_ref, wq_hbm, kv_hbm, wo_hbm, out_ref,
    w_in, w_out, normed, q_s, k_s, v_s, ctx, own_part, sib_out, sib_in, ring_out, relay, arrived,
    load_sem, kv_sem, ag_send, ag_recv, sib_send, sib_recv, ring_send, ring_recv,
):
    pipe = lax.axis_index("pipe")
    tensor = lax.axis_index("tensor")
    core = lax.rem(pipe, 2)
    y = lax.div(tensor, 2)
    z_lo = lax.rem(tensor, 2)
    y_up = lax.rem(y + 1, RING)
    y_far = lax.rem(y + 2, RING)
    y_down = lax.rem(y + 3, RING)
    sibling = (pipe + 1 - 2 * core, tensor)
    up = (pipe, 2 * y_up + z_lo)
    down = (pipe, 2 * y_down + z_lo)

    barrier = pltpu.get_barrier_semaphore()
    for other in (sibling, up, down):
        pl.semaphore_signal(barrier, inc=1, device_id=other, device_id_type=MESH)

    load_q = pltpu.make_async_copy(wq_hbm, w_in.at[:, pl.ds(0, 512)], load_sem.at[0])
    kv_cols = pl.ds(pl.multiple_of(512 + core * 128, 128), 128)
    load_kv = pltpu.make_async_copy(kv_hbm, w_in.at[:, kv_cols], load_sem.at[1])
    load_o = pltpu.make_async_copy(wo_hbm, w_out, load_sem.at[2])
    load_q.start()
    load_kv.start()
    load_o.start()

    def norm_rows(step, carry):
        rows = pl.ds(pl.multiple_of(step * 16, 16), 16)
        x = x_ref[rows, :].astype(jnp.float32)
        scale = lax.rsqrt(jnp.mean(x * x, axis=1, keepdims=True) + 1e-05)
        into = pl.ds(pl.multiple_of(core * ROWS + step * 16, 16), 16)
        normed[y, into, :] = (x * scale * gain_ref[...]).astype(jnp.bfloat16)
        return carry

    lax.fori_loop(0, ROWS // 16, norm_rows, 0)
    pl.semaphore_wait(barrier, 3)

    sends = []

    def send(src, dst, send_sem, recv_sem, device):
        copy = pltpu.make_async_remote_copy(
            src_ref=src, dst_ref=dst, send_sem=send_sem, recv_sem=recv_sem,
            device_id=device, device_id_type=MESH,
        )
        copy.start()
        sends.append(copy)

    def piece(chip, side, half):
        return normed.at[chip, pl.ds(pl.multiple_of(side * ROWS + half * HALF, HALF), HALF), :]

    def gather(chip, side, half, device):
        part = piece(chip, side, half)
        send(part, part, ag_send.at[len(sends)], ag_recv.at[chip, side, half], device)

    def wait_piece(chip, side, half):
        part = piece(chip, side, half)
        pltpu.make_async_remote_copy(
            src_ref=part, dst_ref=part, send_sem=ag_send.at[0], recv_sem=ag_recv.at[chip, side, half],
            device_id=sibling, device_id_type=MESH,
        ).wait_recv()

    other = 1 - core
    gather(y, core, 0, up)
    gather(y, core, 1, down)
    gather(y, core, 0, sibling)
    gather(y, core, 1, sibling)
    gather(y, core, 1, up)
    gather(y, core, 0, down)
    kv_view = w_in.at[:, kv_cols]
    load_kv.wait()
    send(kv_view, kv_view, kv_sem.at[0], kv_sem.at[1], sibling)
    load_q.wait()
    kv_other = w_in.at[:, pl.ds(pl.multiple_of(512 + other * 128, 128), 128)]
    pltpu.make_async_remote_copy(
        src_ref=kv_other, dst_ref=kv_other, send_sem=kv_sem.at[0], recv_sem=kv_sem.at[1],
        device_id=sibling, device_id_type=MESH,
    ).wait_recv()

    def project(chip):
        rows = pl.ds(pl.multiple_of(chip * PAIR, PAIR), PAIR)

        def two_heads(n, carry):
            cols = pl.ds(pl.multiple_of(n * 256, 256), 256)
            res = jnp.dot(normed[chip], w_in[:, cols], preferred_element_type=jnp.float32)
            q_s[2 * n, rows, :] = res[:, :128].astype(jnp.bfloat16)
            q_s[2 * n + 1, rows, :] = res[:, 128:].astype(jnp.bfloat16)
            return carry

        lax.fori_loop(0, 2, two_heads, 0)
        res = jnp.dot(normed[chip], w_in[:, 512:768], preferred_element_type=jnp.float32)
        k_s[rows, :] = jnp.concatenate([res[:, 0:64], res[:, 128:192]], axis=1).astype(jnp.bfloat16)
        v_s[rows, :] = jnp.concatenate([res[:, 64:128], res[:, 192:256]], axis=1).astype(jnp.bfloat16)

    wait_piece(y, other, 0)
    wait_piece(y, other, 1)
    project(y)
    wait_piece(y_down, core, 0)
    gather(y_down, core, 0, up)
    gather(y_down, core, 0, sibling)
    wait_piece(y_up, core, 1)
    gather(y_up, core, 1, down)
    gather(y_up, core, 1, sibling)
    wait_piece(y_down, core, 1)
    gather(y_down, core, 1, sibling)
    wait_piece(y_up, core, 0)
    gather(y_up, core, 0, sibling)
    for chip in (y_down, y_up):
        wait_piece(chip, other, 0)
        wait_piece(chip, other, 1)
        project(chip)
    wait_piece(y_far, core, 0)
    gather(y_far, core, 0, sibling)
    wait_piece(y_far, core, 1)
    gather(y_far, core, 1, sibling)
    wait_piece(y_far, other, 0)
    wait_piece(y_far, other, 1)
    project(y_far)

    scale = HEAD_DIM ** (-0.5)

    def head(h, carry):
        cols = pl.ds(pl.multiple_of(h * HEAD_DIM, HEAD_DIM), HEAD_DIM)
        for i in range(RING):
            keys = PAIR * (i + 1)
            scores = lax.dot_general(
                q_s[h, PAIR * i : keys, :], k_s[:keys, :], (((1,), (1,)), ((), ())),
                preferred_element_type=jnp.float32,
            ) * scale
            q_pos = PAIR * i + lax.broadcasted_iota(jnp.int32, (PAIR, keys), 0)
            k_pos = lax.broadcasted_iota(jnp.int32, (PAIR, keys), 1)
            scores = jnp.where(q_pos >= k_pos, scores, -1e30)
            top = jnp.max(scores, axis=1, keepdims=True)
            exps = jnp.exp(scores - top)
            weights = (exps * (1.0 / jnp.sum(exps, axis=1, keepdims=True))).astype(jnp.bfloat16)
            mixed = jnp.dot(weights, v_s[:keys, :], preferred_element_type=jnp.float32)
            ctx[i, :, cols] = mixed.astype(jnp.bfloat16)
        return carry

    lax.fori_loop(0, HEADS_DEV, head, 0)

    load_o.wait()

    def out_project(slot, chip):
        def columns(n, carry):
            cols = pl.ds(pl.multiple_of(n * 512, 512), 512)
            res = jnp.dot(ctx[chip], w_out[:, cols], preferred_element_type=jnp.float32)
            low, high = res[:ROWS], res[ROWS:]
            own_part[slot, :, cols] = jnp.where(core == 0, low, high)
            sib_out[slot, :, cols] = jnp.where(core == 0, high, low).astype(jnp.bfloat16)
            return carry

        lax.fori_loop(0, WIDTH // 512, columns, 0)
        send(sib_out.at[slot], sib_in.at[slot], sib_send.at[slot], sib_recv.at[slot], sibling)

    def wait_recv(ref, sem):
        pltpu.make_async_remote_copy(
            src_ref=ref, dst_ref=ref, send_sem=sib_send.at[0], recv_sem=sem,
            device_id=sibling, device_id_type=MESH,
        ).wait_recv()

    def combine(slot, first, count, relayed):
        def rows_step(step, carry):
            rows = pl.ds(pl.multiple_of(first + step * 16, 16), 16)
            total = own_part[slot, rows, :] + sib_in[slot, rows, :].astype(jnp.float32)
            if relayed is not None:
                from_rows = pl.ds(pl.multiple_of(step * 16, 16), 16)
                total = total + relay[relayed, from_rows, :].astype(jnp.float32)
            ring_out[slot, rows, :] = total.astype(jnp.bfloat16)
            return carry

        lax.fori_loop(0, count // 16, rows_step, 0)

    out_project(0, y_far)
    out_project(1, y_up)
    wait_recv(sib_in.at[0], sib_recv.at[0])
    combine(0, 0, ROWS, None)
    send(ring_out.at[0, pl.ds(0, HALF)], relay.at[0], ring_send.at[0], ring_recv.at[0], up)
    send(ring_out.at[0, pl.ds(HALF, HALF)], relay.at[1], ring_send.at[1], ring_recv.at[1], down)
    out_project(2, y_down)
    wait_recv(sib_in.at[1], sib_recv.at[1])
    combine(1, HALF, HALF, None)
    send(ring_out.at[1, pl.ds(HALF, HALF)], arrived.at[0, pl.ds(HALF, HALF)], ring_send.at[2], ring_recv.at[2], up)
    wait_recv(sib_in.at[2], sib_recv.at[2])
    combine(2, 0, HALF, None)
    send(ring_out.at[2, pl.ds(0, HALF)], arrived.at[1, pl.ds(0, HALF)], ring_send.at[3], ring_recv.at[3], down)
    out_project(3, y)
    wait_recv(relay.at[0], ring_recv.at[0])
    combine(1, 0, HALF, 0)
    send(ring_out.at[1, pl.ds(0, HALF)], arrived.at[0, pl.ds(0, HALF)], ring_send.at[4], ring_recv.at[4], up)
    wait_recv(relay.at[1], ring_recv.at[1])
    combine(2, HALF, HALF, 1)
    send(ring_out.at[2, pl.ds(HALF, HALF)], arrived.at[1, pl.ds(HALF, HALF)], ring_send.at[5], ring_recv.at[5], down)
    wait_recv(sib_in.at[3], sib_recv.at[3])

    def finish(first):
        def rows_step(step, carry):
            rows = pl.ds(pl.multiple_of(first + step * 16, 16), 16)
            total = own_part[3, rows, :] + sib_in[3, rows, :].astype(jnp.float32)
            total = total + arrived[0, rows, :].astype(jnp.float32)
            total = total + arrived[1, rows, :].astype(jnp.float32)
            out_ref[rows, :] = x_ref[rows, :].astype(jnp.float32) + total
            return carry

        lax.fori_loop(0, HALF // 16, rows_step, 0)

    for sem in (2, 3, 4, 5):
        slot = 0 if sem in (2, 4) else 1
        first = HALF if sem in (2, 5) else 0
        wait_recv(arrived.at[slot, pl.ds(first, HALF)], ring_recv.at[sem])
    finish(0)
    finish(HALF)
    for copy in sends:
        copy.wait_send()


def layer(x, gain, wq, kv, wo):
    bf16, f32 = jnp.bfloat16, jnp.float32
    dma = pltpu.SemaphoreType.DMA
    vmem = pl.BlockSpec(memory_space=pltpu.VMEM)
    hbm = pl.BlockSpec(memory_space=pl.ANY)
    return pl.pallas_call(
        layer_kernel,
        out_shape=jax.ShapeDtypeStruct((ROWS, WIDTH), f32),
        in_specs=[vmem, vmem, hbm, hbm, hbm],
        out_specs=vmem,
        scratch_shapes=[
            pltpu.VMEM((WIDTH, 768), bf16),
            pltpu.VMEM((512, WIDTH), bf16),
            pltpu.VMEM((RING, PAIR, WIDTH), bf16),
            pltpu.VMEM((HEADS_DEV, TOKENS, HEAD_DIM), bf16),
            pltpu.VMEM((TOKENS, HEAD_DIM), bf16),
            pltpu.VMEM((TOKENS, HEAD_DIM), bf16),
            pltpu.VMEM((RING, PAIR, 512), bf16),
            pltpu.VMEM((4, ROWS, WIDTH), f32),
            pltpu.VMEM((4, ROWS, WIDTH), bf16),
            pltpu.VMEM((4, ROWS, WIDTH), bf16),
            pltpu.VMEM((3, ROWS, WIDTH), bf16),
            pltpu.VMEM((2, HALF, WIDTH), bf16),
            pltpu.VMEM((2, ROWS, WIDTH), bf16),
            dma((3,)), dma((2,)), dma((15,)), dma((RING, 2, 2)),
            dma((4,)), dma((4,)), dma((6,)), dma((6,)),
        ],
        compiler_params=pltpu.CompilerParams(
            collective_id=0, has_side_effects=True, vmem_limit_bytes=58 << 20
        ),
        cost_estimate=pl.CostEstimate(flops=12 * 10**9, bytes_accessed=16 << 20, transcendentals=4 << 20),
        name="attention_layer",
    )(x, gain, wq, kv, wo)


def body(
    entry_symbol_ids,
    lookup_table_matrix,
    pending_batches,
    scale_factors,
    query_projector,
    key_projector,
    value_projector,
    result_projector,
):
    pipe_pos = lax.axis_index("pipe")
    tensor_pos = lax.axis_index("tensor")
    section = 2 * (pipe_pos // 2) + tensor_pos % 2
    vocab_dev = lookup_table_matrix.shape[0]
    local_index = entry_symbol_ids - pipe_pos * vocab_dev
    inside = (local_index >= 0) & (local_index < vocab_dev)
    looked = jnp.take(lookup_table_matrix, jnp.clip(local_index, 0, vocab_dev - 1), axis=0)
    looked = jnp.where(inside[:, None], looked, jnp.zeros_like(looked))
    exchanged = lax.all_to_all(
        looked.reshape(8, ROWS, -1), "tensor", split_axis=0, concat_axis=2, tiled=True
    ).reshape(ROWS, WIDTH)
    entering = lax.psum(exchanged.astype(jnp.float32).astype(jnp.bfloat16), "pipe")

    kv = traded(jnp.concatenate([key_projector[0], value_projector[0]], axis=1))
    wq = traded(query_projector[0])
    wo = traded(result_projector[0])
    gain = traded(scale_factors)
    first_in = traded(pending_batches)
    first_out = layer(first_in.astype(jnp.float32), gain, wq, kv, wo)
    passed = to_next_section(first_out)
    second_in = jnp.where(section == 0, traded(entering).astype(jnp.float32), passed)
    second_out = layer(second_in, gain, wq, kv, wo)
    return (traded(first_out), traded(second_out))


def solution(mesh):
    in_specs = (
        P(),
        P("pipe", "tensor"),
        P(("pipe", "tensor"), None),
        P("pipe", None),
        P("pipe", None, "tensor"),
        P("pipe", None, "tensor"),
        P("pipe", None, "tensor"),
        P("pipe", "tensor", None),
    )
    out_specs = (P(("pipe", "tensor"), None), P(("pipe", "tensor"), None))
    return jax.shard_map(body, mesh=mesh, in_specs=in_specs, out_specs=out_specs, check_vma=False)
```

```python
import functools

import jax
import jax.numpy as jnp
from jax import lax
from jax.experimental import pallas as pl
from jax.experimental.pallas import tpu as pltpu
from jax.sharding import PartitionSpec as P

HEAD_DIM = 128
MESH = pl.DeviceIdType.MESH
BOTH = ("pipe", "tensor")
SECTIONS = 16
RING = 4
TOKENS = 1024
ROWS = 128
WIDTH = 4096
COLS = 512
HEADS_DEV = 4
PAIR = 2 * ROWS
HALF = ROWS // 2
PARTS = 8
PART = WIDTH // PARTS


def flat(pipe, tensor):
    return pipe * 8 + tensor


def physical(section, block):
    return flat(2 * (section // 2) + block % 2, 2 * (block // 2) + section % 2)


def traded(array):
    route = [(flat(s, t), physical(s, t)) for s in range(SECTIONS) for t in range(8)]
    return lax.ppermute(array, BOTH, route)


def remote(src, dst, send_sem, recv_sem, device):
    return pltpu.make_async_remote_copy(
        src_ref=src, dst_ref=dst, send_sem=send_sem, recv_sem=recv_sem,
        device_id=device, device_id_type=MESH,
    )


def aligned(start, size):
    return pl.ds(pl.multiple_of(start, size), size)


def layer_kernel(first, *refs):
    if first:
        (x_ref, gain_ref, wq_hbm, kv_hbm, wo_hbm, looked_hbm,
         out_hbm, next_hbm, w_in_hbm, w_out_hbm, *refs) = refs
    else:
        (x_ref, gain_ref, w_in_hbm, w_out_hbm, held_hbm, held_out, out_hbm, *refs) = refs
    (w_in, w_out, normed, q_s, k_s, v_s, ctx, own_part, sib_out, sib_in, ring_out, relay, arrived,
     out_s, load_sem, kv_sem, ag_send, ag_recv, sib_send, sib_recv, ring_send, ring_recv,
     trade_send, trade_recv, out_send, out_recv, *refs) = refs
    if first:
        next_s, e_acc, e_in, e_sem, e_send, e_recv, all_send, all_recv, next_send, next_recv = refs

    pipe = lax.axis_index("pipe")
    tensor = lax.axis_index("tensor")
    core = lax.rem(pipe, 2)
    x_pos = lax.rem(lax.div(pipe, 2), 4)
    z_hi = lax.div(pipe, 8)
    y = lax.div(tensor, 2)
    z_lo = lax.rem(tensor, 2)
    y_up = lax.rem(y + 1, RING)
    y_far = lax.rem(y + 2, RING)
    y_down = lax.rem(y + 3, RING)
    other = 1 - core
    section = pipe - core + z_lo
    sibling = (pipe + 1 - 2 * core, tensor)
    up = (pipe, 2 * y_up + z_lo)
    down = (pipe, 2 * y_down + z_lo)
    stays = core == z_lo
    moves = core != z_lo
    partner = (pipe - core + z_lo, tensor - z_lo + core)
    has_next = section < SECTIONS - 1
    has_prev = section > 0
    after = (pipe + 2 * z_lo, tensor + 1 - 2 * z_lo)
    before = (pipe - 2 * (1 - z_lo), tensor + 1 - 2 * z_lo)

    barrier = pltpu.get_barrier_semaphore()
    greeted = []

    def greet(device, condition=None):
        def signal():
            pl.semaphore_signal(barrier, inc=1, device_id=device, device_id_type=MESH)

        if condition is None:
            signal()
            greeted.append(1)
        else:
            pl.when(condition)(signal)
            greeted.append(jnp.where(condition, 1, 0))

    greet(sibling)
    greet(up)
    greet(down)
    greet(partner, moves)
    if first:
        lead = core == 0
        x_odd = lax.rem(x_pos, 2) == 1
        sends_2 = lead & x_odd
        takes_2 = lead & (lax.rem(x_pos, 2) == 0)
        sends_3 = lead & (x_pos == 2)
        takes_3 = lead & (x_pos == 0)
        sends_4 = lead & (x_pos == 0) & (z_hi == 1)
        is_root = pipe == 0
        enters = (section == 0)
        greet(after, has_next)
        greet(before, has_prev)
        greet((pipe - 2, tensor), sends_2)
        greet((pipe + 2, tensor), takes_2)
        greet((pipe - 4, tensor), sends_3)
        greet((pipe + 4, tensor), takes_3)
        greet((pipe - 8, tensor), sends_4)
        greet((pipe + 8, tensor), is_root)
        for t in range(8):
            is_me = (pipe == t % 2) & (tensor == 2 * (t // 2))
            greet((t % 2, 2 * (t // 2)), is_root & jnp.logical_not(is_me))
            greet((0, t), enters & jnp.logical_not(is_root & (tensor == t)))
        load_looked = pltpu.make_async_copy(looked_hbm, e_acc, e_sem.at[0])
        load_looked.start()
    else:
        load_in = pltpu.make_async_copy(w_in_hbm, w_in, load_sem.at[0])
        load_in.start()
        load_out = pltpu.make_async_copy(w_out_hbm, w_out, load_sem.at[1])
        load_out.start()

    def norm_rows(step, carry):
        x = x_ref[aligned(step * 16, 16), :].astype(jnp.float32)
        scale = lax.rsqrt(jnp.mean(x * x, axis=1, keepdims=True) + 1e-05)
        normed[y, aligned(core * ROWS + step * 16, 16), :] = (x * scale * gain_ref[...]).astype(jnp.bfloat16)
        return carry

    lax.fori_loop(0, ROWS // 16, norm_rows, 0)
    pl.semaphore_wait(barrier, functools.reduce(lambda a, b: a + b, greeted))

    def hand_over(src, dst, slot, sends=trade_send, recvs=trade_recv):
        @pl.when(stays)
        def _():
            pltpu.make_async_copy(src, dst, recvs.at[slot]).start()

        @pl.when(moves)
        def _():
            remote(src, dst, sends.at[slot], recvs.at[slot], partner).start()

    def handed(src, dst, slot, sends=trade_send, recvs=trade_recv):
        remote(src, dst, sends.at[slot], recvs.at[slot], partner).wait_recv()

    def handed_over(src, dst, slot, sends=trade_send, recvs=trade_recv):
        @pl.when(moves)
        def _():
            remote(src, dst, sends.at[slot], recvs.at[slot], partner).wait_send()

    sends = []

    def piece(chip, side, half):
        return normed.at[chip, aligned(side * ROWS + half * HALF, HALF), :]

    def gather(chip, side, half, device):
        part = piece(chip, side, half)
        copy = remote(part, part, ag_send.at[len(sends)], ag_recv.at[chip, side, half], device)
        copy.start()
        sends.append(copy)

    def wait_piece(chip, side, half):
        part = piece(chip, side, half)
        remote(part, part, ag_send.at[0], ag_recv.at[chip, side, half], sibling).wait_recv()

    gather(y, core, 0, up)
    gather(y, core, 1, down)
    gather(y, core, 0, sibling)
    gather(y, core, 1, sibling)
    gather(y, core, 1, up)
    gather(y, core, 0, down)

    def forward_near():
        wait_piece(y_down, core, 0)
        gather(y_down, core, 0, up)
        gather(y_down, core, 0, sibling)
        wait_piece(y_up, core, 1)
        gather(y_up, core, 1, down)
        gather(y_up, core, 1, sibling)
        wait_piece(y_down, core, 1)
        gather(y_down, core, 1, sibling)
        wait_piece(y_up, core, 0)
        gather(y_up, core, 0, sibling)

    def forward_far():
        wait_piece(y_far, core, 0)
        gather(y_far, core, 0, sibling)
        wait_piece(y_far, core, 1)
        gather(y_far, core, 1, sibling)

    def project(chip):
        rows = aligned(chip * PAIR, PAIR)

        def two_heads(n, carry):
            res = jnp.dot(normed[chip], w_in[:, aligned(n * 256, 256)], preferred_element_type=jnp.float32)
            q_s[2 * n, rows, :] = res[:, :128].astype(jnp.bfloat16)
            q_s[2 * n + 1, rows, :] = res[:, 128:].astype(jnp.bfloat16)
            return carry

        lax.fori_loop(0, 2, two_heads, 0)
        res = jnp.dot(normed[chip], w_in[:, 512:768], preferred_element_type=jnp.float32)
        k_s[rows, :] = jnp.concatenate([res[:, 0:64], res[:, 128:192]], axis=1).astype(jnp.bfloat16)
        v_s[rows, :] = jnp.concatenate([res[:, 64:128], res[:, 192:256]], axis=1).astype(jnp.bfloat16)

    def out_cols(n):
        return aligned(n * PART, PART)

    if first:
        kv_own = w_in.at[:, aligned(512 + core * 128, 128)]
        kv_partner = w_in.at[:, aligned(512 + z_lo * 128, 128)]
        kv_rest = w_in.at[:, aligned(512 + other * 128, 128)]
        wq_slot = w_in.at[:, pl.ds(0, 512)]

        def wo_part(n):
            return (wo_hbm.at[:, out_cols(n)], w_out.at[:, out_cols(n)], 2 + n)

        hand_over(kv_hbm, kv_partner, 0)
        hand_over(wq_hbm, wq_slot, 1)

        def tree(slot, src, device):
            return remote(src, e_in.at[slot], e_send.at[slot], e_recv.at[slot], device)

        def add_in(slot):
            tree(slot, e_acc, sibling).wait_recv()

            def rows_step(step, carry):
                rows = aligned(step * 64, 64)
                e_acc[rows, :] = e_acc[rows, :] + e_in[slot, rows, :]
                return carry

            lax.fori_loop(0, TOKENS // 64, rows_step, 0)

        load_looked.wait()

        @pl.when(core == 1)
        def _():
            tree(0, e_acc, sibling).start()

        @pl.when(lead)
        def _():
            add_in(0)

        @pl.when(sends_2)
        def _():
            tree(1, e_acc, (pipe - 2, tensor)).start()

        forward_near()

        @pl.when(takes_2)
        def _():
            add_in(1)

        @pl.when(sends_3)
        def _():
            tree(2, e_acc, (pipe - 4, tensor)).start()

        forward_far()

        @pl.when(takes_3)
        def _():
            add_in(2)

        @pl.when(sends_4)
        def _():
            tree(3, e_acc, (pipe - 8, tensor)).start()

        handed(kv_hbm, kv_own, 0)
        share = remote(kv_own, kv_own, kv_sem.at[0], kv_sem.at[1], sibling)
        share.start()
        handed(wq_hbm, wq_slot, 1)
        handed_over(kv_hbm, kv_partner, 0)
        handed_over(wq_hbm, wq_slot, 1)
        for n in range(2):
            hand_over(*wo_part(n))
        remote(kv_rest, kv_rest, kv_sem.at[0], kv_sem.at[1], sibling).wait_recv()
        keep_in = pltpu.make_async_copy(w_in, w_in_hbm, load_sem.at[0])
        keep_in.start()
        for chip in range(RING):
            for side in range(2):
                @pl.when((side != core) | False)
                def _(chip=chip, side=side):
                    wait_piece(chip, side, 0)
                    wait_piece(chip, side, 1)

        def project_step(chip, carry):
            project(chip)
            return carry

        lax.fori_loop(0, RING, project_step, 0)
    else:
        held_src = held_hbm
        hand_over(held_src, held_out, 0)
        wait_piece(y, other, 0)
        wait_piece(y, other, 1)
        load_in.wait()
        project(y)
        forward_near()
        for chip in (y_down, y_up):
            wait_piece(chip, other, 0)
            wait_piece(chip, other, 1)
            project(chip)
        forward_far()
        wait_piece(y_far, other, 0)
        wait_piece(y_far, other, 1)
        project(y_far)

    scale = HEAD_DIM ** (-0.5)

    def head(h, carry):
        cols = aligned(h * HEAD_DIM, HEAD_DIM)
        for i in range(RING):
            keys = PAIR * (i + 1)
            scores = lax.dot_general(
                q_s[h, PAIR * i : keys, :], k_s[:keys, :], (((1,), (1,)), ((), ())),
                preferred_element_type=jnp.float32,
            ) * scale
            q_pos = PAIR * i + lax.broadcasted_iota(jnp.int32, (PAIR, keys), 0)
            k_pos = lax.broadcasted_iota(jnp.int32, (PAIR, keys), 1)
            scores = jnp.where(q_pos >= k_pos, scores, -1e30)
            top = jnp.max(scores, axis=1, keepdims=True)
            exps = jnp.exp(scores - top)
            weights = (exps * (1.0 / jnp.sum(exps, axis=1, keepdims=True))).astype(jnp.bfloat16)
            mixed = jnp.dot(weights, v_s[:keys, :], preferred_element_type=jnp.float32)
            ctx[i, :, cols] = mixed.astype(jnp.bfloat16)
        return carry

    lax.fori_loop(0, HEADS_DEV, head, 0)

    if first:
        def spread(t, column):
            return (
                e_acc.at[pl.ds(t * ROWS, ROWS), :],
                next_hbm.at[:, aligned(column * COLS, COLS)],
            )

        @pl.when(is_root)
        def _():
            add_in(3)
            for t in range(8):
                src, dst = spread(t, tensor)
                is_me = (t % 2 == 0) & (tensor == 2 * (t // 2))

                @pl.when(is_me)
                def _(src=src, dst=dst):
                    pltpu.make_async_copy(src, dst, all_recv.at[tensor]).start()

                @pl.when(jnp.logical_not(is_me))
                def _(src=src, dst=dst, t=t):
                    remote(src, dst, all_send.at[t], all_recv.at[tensor], (t % 2, 2 * (t // 2))).start()

    def sib_copy(n):
        return remote(sib_out.at[n], sib_in.at[n], sib_send.at[n], sib_recv.at[n], sibling)

    low, high = pl.ds(0, HALF), pl.ds(HALF, HALF)
    ring_plan = (
        (0, low, "relay", 0, up),
        (0, high, "relay", 1, down),
        (1, high, "arrived", 0, up),
        (2, low, "arrived", 1, down),
        (1, low, "arrived", 0, up),
        (2, high, "arrived", 1, down),
    )

    def ring_copy(n, index):
        slot, rows, into, side, device = ring_plan[index]
        dst = relay.at[n, side] if into == "relay" else arrived.at[n, side, rows]
        return remote(ring_out.at[n, slot, rows], dst, ring_send.at[n, index], ring_recv.at[n, index], device)

    def combine(n, slot, ring_slot, first_row, count, relayed):
        def rows_step(step, carry):
            rows = aligned(first_row + step * 16, 16)
            total = own_part[n, slot, rows, :] + sib_in[n, slot, rows, :].astype(jnp.float32)
            if relayed is not None:
                total = total + relay[n, relayed, aligned(step * 16, 16), :].astype(jnp.float32)
            ring_out[n, ring_slot, rows, :] = total.astype(jnp.bfloat16)
            return carry

        lax.fori_loop(0, count // 16, rows_step, 0)

    def project_part(n):
        if first:
            handed(*wo_part(n))
            handed_over(*wo_part(n))

            @pl.when(n < PARTS - 2)
            def _():
                hand_over(*wo_part(n + 2))

        def slot_step(slot, carry):
            chip = lax.rem(y + 6 - slot, RING)
            res = jnp.dot(ctx[chip], w_out[:, out_cols(n)], preferred_element_type=jnp.float32)
            top, bottom = res[:ROWS], res[ROWS:]
            own_part[n, slot] = jnp.where(core == 0, top, bottom)
            sib_out[n, slot] = jnp.where(core == 0, bottom, top).astype(jnp.bfloat16)
            return carry

        lax.fori_loop(0, 4, slot_step, 0)
        sib_copy(n).start()

    def send_part(n):
        sib_copy(n).wait_recv()
        combine(n, 0, 0, 0, ROWS, None)
        ring_copy(n, 0).start()
        ring_copy(n, 1).start()
        combine(n, 1, 1, HALF, HALF, None)
        ring_copy(n, 2).start()
        combine(n, 3, 2, 0, HALF, None)
        ring_copy(n, 3).start()

    def relay_part(n):
        ring_copy(n, 0).wait_recv()
        combine(n, 1, 1, 0, HALF, 0)
        ring_copy(n, 4).start()
        ring_copy(n, 1).wait_recv()
        combine(n, 3, 2, HALF, HALF, 1)
        ring_copy(n, 5).start()

    def next_copy(n, device):
        return remote(next_s.at[n], next_hbm.at[:, out_cols(n)], next_send.at[n], next_recv.at[n], device)

    def out_part(n):
        return (out_s.at[n], out_hbm.at[:, out_cols(n)], n)

    def finish_part(n):
        for index in (2, 3, 4, 5):
            ring_copy(n, index).wait_recv()

        def rows_step(step, carry):
            rows = aligned(step * 16, 16)
            total = own_part[n, 2, rows, :] + sib_in[n, 2, rows, :].astype(jnp.float32)
            total = total + arrived[n, 0, rows, :].astype(jnp.float32)
            total = total + arrived[n, 1, rows, :].astype(jnp.float32)
            total = x_ref[rows, out_cols(n)].astype(jnp.float32) + total
            out_s[n, rows, :] = total
            if first:
                next_s[n, rows, :] = total.astype(jnp.bfloat16)
            return carry

        lax.fori_loop(0, ROWS // 16, rows_step, 0)
        if first:
            @pl.when(has_next)
            def _():
                next_copy(n, after).start()

            pltpu.make_async_copy(out_s.at[n], out_hbm.at[:, out_cols(n)], out_recv.at[n]).start()
        else:
            hand_over(*out_part(n), out_send, out_recv)

    if not first:
        load_out.wait()

    def pipeline(i, carry):
        @pl.when(i < PARTS)
        def _():
            project_part(i)

        @pl.when((i >= 1) & (i < PARTS + 1))
        def _():
            send_part(i - 1)

        @pl.when((i >= 2) & (i < PARTS + 2))
        def _():
            relay_part(i - 2)

        @pl.when(i >= 3)
        def _():
            finish_part(i - 3)

        return carry

    lax.fori_loop(0, PARTS + 3, pipeline, 0)

    if first:
        keep_out = pltpu.make_async_copy(w_out, w_out_hbm, load_sem.at[1])
        keep_out.start()
        share.wait_send()
        keep_in.wait()
        keep_out.wait()

        @pl.when(core == 1)
        def _():
            tree(0, e_acc, sibling).wait_send()

        @pl.when(sends_2)
        def _():
            tree(1, e_acc, (pipe - 2, tensor)).wait_send()

        @pl.when(sends_3)
        def _():
            tree(2, e_acc, (pipe - 4, tensor)).wait_send()

        @pl.when(sends_4)
        def _():
            tree(3, e_acc, (pipe - 8, tensor)).wait_send()

        @pl.when(is_root)
        def _():
            for t in range(8):
                src, dst = spread(t, tensor)

                @pl.when(jnp.logical_not((t % 2 == 0) & (tensor == 2 * (t // 2))))
                def _(src=src, dst=dst, t=t):
                    remote(src, dst, all_send.at[t], all_recv.at[tensor], (t % 2, 2 * (t // 2))).wait_send()

        @pl.when(enters)
        def _():
            for t in range(8):
                src, dst = spread(0, t)
                remote(src, dst, all_send.at[0], all_recv.at[t], sibling).wait_recv()

    else:
        handed(held_src, held_out, 0)
        handed_over(held_src, held_out, 0)

    for copy in sends:
        copy.wait_send()

    def drain(n, carry):
        sib_copy(n).wait_send()
        for index in range(6):
            ring_copy(n, index).wait_send()
        if first:
            @pl.when(has_next)
            def _():
                next_copy(n, after).wait_send()

            @pl.when(has_prev)
            def _():
                next_copy(n, after).wait_recv()

            pltpu.make_async_copy(out_s.at[n], out_hbm.at[:, out_cols(n)], out_recv.at[n]).wait()
        else:
            handed(*out_part(n), out_send, out_recv)
            handed_over(*out_part(n), out_send, out_recv)
        return carry

    lax.fori_loop(0, PARTS, drain, 0)


def layer(first, *operands):
    bf16, f32 = jnp.bfloat16, jnp.float32
    dma = pltpu.SemaphoreType.DMA
    vmem = pl.BlockSpec(memory_space=pltpu.VMEM)
    hbm = pl.BlockSpec(memory_space=pl.ANY)
    block = jax.ShapeDtypeStruct((ROWS, WIDTH), f32)
    if first:
        out_shape = (
            block,
            jax.ShapeDtypeStruct((ROWS, WIDTH), bf16),
            jax.ShapeDtypeStruct((WIDTH, 768), bf16),
            jax.ShapeDtypeStruct((512, WIDTH), bf16),
        )
    else:
        out_shape = (block, block)
    scratch = [
        pltpu.VMEM((WIDTH, 768), bf16),
        pltpu.VMEM((512, WIDTH), bf16),
        pltpu.VMEM((RING, PAIR, WIDTH), bf16),
        pltpu.VMEM((HEADS_DEV, TOKENS, HEAD_DIM), bf16),
        pltpu.VMEM((TOKENS, HEAD_DIM), bf16),
        pltpu.VMEM((TOKENS, HEAD_DIM), bf16),
        pltpu.VMEM((RING, PAIR, 512), bf16),
        pltpu.VMEM((PARTS, 4, ROWS, PART), f32),
        pltpu.VMEM((PARTS, 4, ROWS, PART), bf16),
        pltpu.VMEM((PARTS, 4, ROWS, PART), bf16),
        pltpu.VMEM((PARTS, 3, ROWS, PART), bf16),
        pltpu.VMEM((PARTS, 2, HALF, PART), bf16),
        pltpu.VMEM((PARTS, 2, ROWS, PART), bf16),
        pltpu.VMEM((PARTS, ROWS, PART), f32),
        dma((2,)), dma((2,)), dma((14,)), dma((RING, 2, 2)),
        dma((PARTS,)), dma((PARTS,)), dma((PARTS, 6)), dma((PARTS, 6)),
        dma((2 + PARTS,)), dma((2 + PARTS,)), dma((PARTS,)), dma((PARTS,)),
    ]
    if first:
        scratch += [
            pltpu.VMEM((PARTS, ROWS, PART), bf16),
            pltpu.VMEM((TOKENS, COLS), bf16),
            pltpu.VMEM((4, TOKENS, COLS), bf16),
            dma((1,)), dma((4,)), dma((4,)), dma((8,)), dma((8,)), dma((PARTS,)), dma((PARTS,)),
        ]
    return pl.pallas_call(
        functools.partial(layer_kernel, first),
        out_shape=out_shape,
        in_specs=[vmem, vmem] + [hbm] * (len(operands) - 2),
        out_specs=tuple(hbm for _ in out_shape),
        scratch_shapes=scratch,
        compiler_params=pltpu.CompilerParams(
            collective_id=0 if first else 1, has_side_effects=True, vmem_limit_bytes=60 << 20
        ),
        cost_estimate=pl.CostEstimate(flops=12 * 10**9, bytes_accessed=16 << 20, transcendentals=4 << 20),
        name="first_layer" if first else "second_layer",
    )(*operands)


def body(
    entry_symbol_ids,
    lookup_table_matrix,
    pending_batches,
    scale_factors,
    query_projector,
    key_projector,
    value_projector,
    result_projector,
):
    pipe_pos = lax.axis_index("pipe")
    vocab_dev = lookup_table_matrix.shape[0]
    local_index = entry_symbol_ids - pipe_pos * vocab_dev
    inside = (local_index >= 0) & (local_index < vocab_dev)
    looked = jnp.take(lookup_table_matrix, jnp.clip(local_index, 0, vocab_dev - 1), axis=0)
    looked = jnp.where(inside[:, None], looked, jnp.zeros_like(looked))
    kv = jnp.concatenate([key_projector[0], value_projector[0]], axis=1)
    gain = traded(scale_factors)
    first_in = traded(pending_batches)
    first_held, second_in, w_in, w_out = layer(
        True, first_in, gain, query_projector[0], kv, result_projector[0], looked
    )
    return layer(False, second_in, gain, w_in, w_out, first_held)


def solution(mesh):
    in_specs = (
        P(),
        P("pipe", "tensor"),
        P(("pipe", "tensor"), None),
        P("pipe", None),
        P("pipe", None, "tensor"),
        P("pipe", None, "tensor"),
        P("pipe", None, "tensor"),
        P("pipe", "tensor", None),
    )
    out_specs = (P(("pipe", "tensor"), None), P(("pipe", "tensor"), None))
    return jax.shard_map(body, mesh=mesh, in_specs=in_specs, out_specs=out_specs, check_vma=False)
```

```python
import functools

import jax
import jax.numpy as jnp
from jax import lax
from jax.experimental import pallas as pl
from jax.experimental.pallas import tpu as pltpu
from jax.sharding import PartitionSpec as P

HEAD_DIM = 128
MESH = pl.DeviceIdType.MESH
BOTH = ("pipe", "tensor")
SECTIONS = 16
RING = 4
TOKENS = 1024
ROWS = 128
WIDTH = 4096
COLS = 512
HEADS_DEV = 4
PAIR = 2 * ROWS
HALF = ROWS // 2
PARTS = 8
PART = WIDTH // PARTS
AHEAD = 3


def flat(pipe, tensor):
    return pipe * 8 + tensor


def physical(section, block):
    return flat(2 * (section // 2) + block % 2, 2 * (block // 2) + section % 2)


def from_partner(array):
    route = [(flat(s, t), physical(s, t)) for s in range(SECTIONS) for t in range(8)]
    return lax.ppermute(array, BOTH, [(a, b) for a, b in route if a != b])


def remote(src, dst, send_sem, recv_sem, device):
    return pltpu.make_async_remote_copy(
        src_ref=src, dst_ref=dst, send_sem=send_sem, recv_sem=recv_sem,
        device_id=device, device_id_type=MESH,
    )


def aligned(start, size):
    return pl.ds(pl.multiple_of(start, size), size)


def layer_kernel(first, *refs):
    if first:
        (x_hbm, x_got_hbm, gain_hbm, wq_hbm, wk_hbm, wv_hbm, wo_hbm, looked_hbm,
         out_hbm, next_hbm, gain_keep, wq_keep, kv_keep, wo_keep, *refs) = refs
    else:
        (x_hbm, gain_hbm, wq_hbm, kv_hbm, wo_hbm, held_hbm, held_out, out_hbm, *refs) = refs
    (x_ref, gain_ref, w_q, w_kv, w_out, normed, q_s, k_s, v_s, ctx, own_part, sib_out, sib_in, ring_out, relay, arrived,
     out_s, load_sem, wo_sem, kv_sem, ag_send, ag_recv, sib_send, sib_recv, ring_send, ring_recv,
     trade_send, trade_recv, out_send, out_recv, *refs) = refs
    if first:
        next_s, e_acc, e_in, e_sem, e_send, e_recv, all_send, all_recv, next_send, next_recv = refs

    pipe = lax.axis_index("pipe")
    tensor = lax.axis_index("tensor")
    core = lax.rem(pipe, 2)
    x_pos = lax.rem(lax.div(pipe, 2), 4)
    z_hi = lax.div(pipe, 8)
    y = lax.div(tensor, 2)
    z_lo = lax.rem(tensor, 2)
    y_up = lax.rem(y + 1, RING)
    y_far = lax.rem(y + 2, RING)
    y_down = lax.rem(y + 3, RING)
    other = 1 - core
    section = pipe - core + z_lo
    sibling = (pipe + 1 - 2 * core, tensor)
    up = (pipe, 2 * y_up + z_lo)
    down = (pipe, 2 * y_down + z_lo)
    stays = core == z_lo
    moves = core != z_lo
    partner = (pipe - core + z_lo, tensor - z_lo + core)
    has_next = section < SECTIONS - 1
    has_prev = section > 0
    after = (pipe + 2 * z_lo, tensor + 1 - 2 * z_lo)
    before = (pipe - 2 * (1 - z_lo), tensor + 1 - 2 * z_lo)

    barrier = pltpu.get_barrier_semaphore()
    greeted = []

    def greet(device, condition=None):
        def signal():
            pl.semaphore_signal(barrier, inc=1, device_id=device, device_id_type=MESH)

        if condition is None:
            signal()
            greeted.append(1)
        else:
            pl.when(condition)(signal)
            greeted.append(jnp.where(condition, 1, 0))

    greet(sibling)
    greet(up)
    greet(down)
    greet(partner, moves)
    if first:
        lead = core == 0
        x_odd = lax.rem(x_pos, 2) == 1
        sends_2 = lead & x_odd
        takes_2 = lead & (lax.rem(x_pos, 2) == 0)
        sends_3 = lead & (x_pos == 2)
        takes_3 = lead & (x_pos == 0)
        sends_4 = lead & (x_pos == 0) & (z_hi == 1)
        is_root = pipe == 0
        enters = (section == 0)
        greet(after, has_next)
        greet(before, has_prev)
        greet((pipe - 2, tensor), sends_2)
        greet((pipe + 2, tensor), takes_2)
        greet((pipe - 4, tensor), sends_3)
        greet((pipe + 4, tensor), takes_3)
        greet((pipe - 8, tensor), sends_4)
        greet((pipe + 8, tensor), is_root)
        for t in range(8):
            is_me = (pipe == t % 2) & (tensor == 2 * (t // 2))
            greet((t % 2, 2 * (t // 2)), is_root & jnp.logical_not(is_me))
            greet((0, t), enters & jnp.logical_not(is_root & (tensor == t)))
        load_looked = pltpu.make_async_copy(looked_hbm, e_acc, e_sem.at[0])
        load_looked.start()

        @pl.when(stays)
        def _():
            pltpu.make_async_copy(x_hbm, x_ref, load_sem.at[0]).start()

        @pl.when(moves)
        def _():
            pltpu.make_async_copy(x_got_hbm, x_ref, load_sem.at[0]).start()

    else:
        load_gain = pltpu.make_async_copy(gain_hbm, gain_ref, load_sem.at[1])
        load_gain.start()
        pltpu.make_async_copy(x_hbm, x_ref, load_sem.at[0]).start()
        load_q = pltpu.make_async_copy(wq_hbm, w_q, load_sem.at[2])
        load_q.start()
        load_kv = pltpu.make_async_copy(kv_hbm, w_kv, load_sem.at[3])
        load_kv.start()
        load_out = pltpu.make_async_copy(wo_hbm, w_out, load_sem.at[4])
        load_out.start()

    pl.semaphore_wait(barrier, functools.reduce(lambda a, b: a + b, greeted))

    def hand_over(src, dst, slot, sends=trade_send, recvs=trade_recv):
        @pl.when(stays)
        def _():
            pltpu.make_async_copy(src, dst, recvs.at[slot]).start()

        @pl.when(moves)
        def _():
            remote(src, dst, sends.at[slot], recvs.at[slot], partner).start()

    def handed(src, dst, slot, sends=trade_send, recvs=trade_recv):
        remote(src, dst, sends.at[slot], recvs.at[slot], partner).wait_recv()

    def handed_over(src, dst, slot, sends=trade_send, recvs=trade_recv):
        @pl.when(moves)
        def _():
            remote(src, dst, sends.at[slot], recvs.at[slot], partner).wait_send()

    def kv_rows(base, block):
        return w_kv.at[aligned(base + block * 64, 64), :]

    if first:
        kv_mine = (kv_rows(0, core), kv_rows(128, core))
        kv_partner = (kv_rows(0, z_lo), kv_rows(128, z_lo))
        kv_rest = (kv_rows(0, other), kv_rows(128, other))
        hand_over(gain_hbm, gain_ref, 0)
        hand_over(wk_hbm, kv_partner[0], 1)
        hand_over(wv_hbm, kv_partner[1], 2)
        hand_over(wq_hbm, w_q, 3)
        handed(gain_hbm, gain_ref, 0)
        keep_gain = pltpu.make_async_copy(gain_ref, gain_keep, load_sem.at[1])
        keep_gain.start()
    else:
        load_gain.wait()
    pltpu.make_async_copy(x_hbm, x_ref, load_sem.at[0]).wait()

    def norm_rows(step, carry):
        x = x_ref[aligned(step * 16, 16), :].astype(jnp.float32)
        scale = lax.rsqrt(jnp.mean(x * x, axis=1, keepdims=True) + 1e-05)
        normed[y, aligned(core * ROWS + step * 16, 16), :] = (x * scale * gain_ref[...]).astype(jnp.bfloat16)
        return carry

    lax.fori_loop(0, ROWS // 16, norm_rows, 0)
    sends = []

    def piece(chip, side, half):
        return normed.at[chip, aligned(side * ROWS + half * HALF, HALF), :]

    def gather(chip, side, half, device):
        part = piece(chip, side, half)
        copy = remote(part, part, ag_send.at[len(sends)], ag_recv.at[chip, side, half], device)
        copy.start()
        sends.append(copy)

    def wait_piece(chip, side, half):
        part = piece(chip, side, half)
        remote(part, part, ag_send.at[0], ag_recv.at[chip, side, half], sibling).wait_recv()

    gather(y, core, 0, up)
    gather(y, core, 1, down)
    gather(y, core, 0, sibling)
    gather(y, core, 1, sibling)
    gather(y, core, 1, up)
    gather(y, core, 0, down)

    def forward_near():
        wait_piece(y_down, core, 0)
        gather(y_down, core, 0, up)
        gather(y_down, core, 0, sibling)
        wait_piece(y_up, core, 1)
        gather(y_up, core, 1, down)
        gather(y_up, core, 1, sibling)
        wait_piece(y_down, core, 1)
        gather(y_down, core, 1, sibling)
        wait_piece(y_up, core, 0)
        gather(y_up, core, 0, sibling)

    def forward_far():
        wait_piece(y_far, core, 0)
        gather(y_far, core, 0, sibling)
        wait_piece(y_far, core, 1)
        gather(y_far, core, 1, sibling)

    def project(chip):
        rows = aligned(chip * PAIR, PAIR)

        def two_heads(n, carry):
            res = jnp.dot(normed[chip], w_q[:, aligned(n * 256, 256)], preferred_element_type=jnp.float32)
            q_s[2 * n, rows, :] = res[:, :128].astype(jnp.bfloat16)
            q_s[2 * n + 1, rows, :] = res[:, 128:].astype(jnp.bfloat16)
            return carry

        lax.fori_loop(0, 2, two_heads, 0)
        res = lax.dot_general(
            normed[chip], w_kv[...], (((1,), (1,)), ((), ())), preferred_element_type=jnp.float32
        )
        k_s[rows, :] = res[:, :128].astype(jnp.bfloat16)
        v_s[rows, :] = res[:, 128:].astype(jnp.bfloat16)

    def out_cols(n):
        return aligned(n * PART, PART)

    if first:
        def wo_part(n):
            return (wo_hbm.at[:, out_cols(n)], w_out.at[:, out_cols(n)], 4 + n)

        def keep_part(n):
            return pltpu.make_async_copy(w_out.at[:, out_cols(n)], wo_keep.at[:, out_cols(n)], wo_sem.at[n])

        def advance(n):
            handed_over(*wo_part(n))

            @pl.when(n < PARTS - AHEAD)
            def _():
                hand_over(*wo_part(n + AHEAD))

        def tree(slot, src, device):
            return remote(src, e_in.at[slot], e_send.at[slot], e_recv.at[slot], device)

        def add_in(slot):
            tree(slot, e_acc, sibling).wait_recv()

            def rows_step(step, carry):
                rows = aligned(step * 64, 64)
                e_acc[rows, :] = e_acc[rows, :] + e_in[slot, rows, :]
                return carry

            lax.fori_loop(0, TOKENS // 64, rows_step, 0)

        load_looked.wait()

        @pl.when(core == 1)
        def _():
            tree(0, e_acc, sibling).start()

        @pl.when(lead)
        def _():
            add_in(0)

        @pl.when(sends_2)
        def _():
            tree(1, e_acc, (pipe - 2, tensor)).start()

        forward_near()

        @pl.when(takes_2)
        def _():
            add_in(1)

        @pl.when(sends_3)
        def _():
            tree(2, e_acc, (pipe - 4, tensor)).start()

        forward_far()

        @pl.when(takes_3)
        def _():
            add_in(2)

        @pl.when(sends_4)
        def _():
            tree(3, e_acc, (pipe - 8, tensor)).start()

        shares = []
        for i in range(2):
            handed((wk_hbm, wv_hbm)[i], kv_mine[i], 1 + i)
            shares.append(remote(kv_mine[i], kv_mine[i], kv_sem.at[i], kv_sem.at[2 + i], sibling))
            shares[i].start()
        handed_over(wq_hbm, w_q, 3)
        for n in range(AHEAD):
            hand_over(*wo_part(n))
        handed(wq_hbm, w_q, 3)
        for i in range(2):
            remote(kv_rest[i], kv_rest[i], kv_sem.at[i], kv_sem.at[2 + i], sibling).wait_recv()
        keep_q = pltpu.make_async_copy(w_q, wq_keep, load_sem.at[2])
        keep_q.start()
        keep_kv = pltpu.make_async_copy(w_kv, kv_keep, load_sem.at[3])
        keep_kv.start()
        for chip in range(RING):
            for side in range(2):
                @pl.when(core != side)
                def _(chip=chip, side=side):
                    wait_piece(chip, side, 0)
                    wait_piece(chip, side, 1)

        def project_step(chip, carry):
            project(chip)
            return carry

        lax.fori_loop(0, RING, project_step, 0)
    else:
        held_src = held_hbm
        hand_over(held_src, held_out, 0)
        wait_piece(y, other, 0)
        wait_piece(y, other, 1)
        load_q.wait()
        load_kv.wait()
        project(y)
        forward_near()
        for chip in (y_down, y_up):
            wait_piece(chip, other, 0)
            wait_piece(chip, other, 1)
            project(chip)
        forward_far()
        wait_piece(y_far, other, 0)
        wait_piece(y_far, other, 1)
        project(y_far)

    scale = HEAD_DIM ** (-0.5)

    def head(h, carry):
        cols = aligned(h * HEAD_DIM, HEAD_DIM)
        for i in range(RING):
            keys = PAIR * (i + 1)
            scores = lax.dot_general(
                q_s[h, PAIR * i : keys, :], k_s[:keys, :], (((1,), (1,)), ((), ())),
                preferred_element_type=jnp.float32,
            ) * scale
            q_pos = PAIR * i + lax.broadcasted_iota(jnp.int32, (PAIR, keys), 0)
            k_pos = lax.broadcasted_iota(jnp.int32, (PAIR, keys), 1)
            scores = jnp.where(q_pos >= k_pos, scores, -1e30)
            top = jnp.max(scores, axis=1, keepdims=True)
            exps = jnp.exp(scores - top)
            weights = (exps * (1.0 / jnp.sum(exps, axis=1, keepdims=True))).astype(jnp.bfloat16)
            mixed = jnp.dot(weights, v_s[:keys, :], preferred_element_type=jnp.float32)
            ctx[i, :, cols] = mixed.astype(jnp.bfloat16)
        if first:
            advance(h)
        return carry

    lax.fori_loop(0, HEADS_DEV, head, 0)

    if first:
        def spread(t, column):
            return (
                e_acc.at[pl.ds(t * ROWS, ROWS), :],
                next_hbm.at[:, aligned(column * COLS, COLS)],
            )

        @pl.when(is_root)
        def _():
            add_in(3)
            for t in range(8):
                src, dst = spread(t, tensor)
                is_me = (t % 2 == 0) & (tensor == 2 * (t // 2))

                @pl.when(is_me)
                def _(src=src, dst=dst):
                    pltpu.make_async_copy(src, dst, all_recv.at[tensor]).start()

                @pl.when(jnp.logical_not(is_me))
                def _(src=src, dst=dst, t=t):
                    remote(src, dst, all_send.at[t], all_recv.at[tensor], (t % 2, 2 * (t // 2))).start()

    def sib_copy(n):
        return remote(sib_out.at[n], sib_in.at[n], sib_send.at[n], sib_recv.at[n], sibling)

    low, high = pl.ds(0, HALF), pl.ds(HALF, HALF)
    ring_plan = (
        (0, low, "relay", 0, up),
        (0, high, "relay", 1, down),
        (1, high, "arrived", 0, up),
        (2, low, "arrived", 1, down),
        (1, low, "arrived", 0, up),
        (2, high, "arrived", 1, down),
    )

    def ring_copy(n, index):
        slot, rows, into, side, device = ring_plan[index]
        dst = relay.at[n, side] if into == "relay" else arrived.at[n, side, rows]
        return remote(ring_out.at[n, slot, rows], dst, ring_send.at[n, index], ring_recv.at[n, index], device)

    def combine(n, slot, ring_slot, first_row, count, relayed):
        def rows_step(step, carry):
            rows = aligned(first_row + step * 16, 16)
            total = own_part[n, slot, rows, :] + sib_in[n, slot, rows, :].astype(jnp.float32)
            if relayed is not None:
                total = total + relay[n, relayed, aligned(step * 16, 16), :].astype(jnp.float32)
            ring_out[n, ring_slot, rows, :] = total.astype(jnp.bfloat16)
            return carry

        lax.fori_loop(0, count // 16, rows_step, 0)

    def project_part(n):
        if first:
            handed(*wo_part(n))
            keep_part(n).start()

            @pl.when(n >= HEADS_DEV)
            def _():
                advance(n)

        def slot_step(slot, carry):
            chip = lax.rem(y + 6 - slot, RING)
            res = jnp.dot(ctx[chip], w_out[:, out_cols(n)], preferred_element_type=jnp.float32)
            top, bottom = res[:ROWS], res[ROWS:]
            own_part[n, slot] = jnp.where(core == 0, top, bottom)
            sib_out[n, slot] = jnp.where(core == 0, bottom, top).astype(jnp.bfloat16)
            return carry

        lax.fori_loop(0, 4, slot_step, 0)
        sib_copy(n).start()

    def send_part(n):
        sib_copy(n).wait_recv()
        combine(n, 0, 0, 0, ROWS, None)
        ring_copy(n, 0).start()
        ring_copy(n, 1).start()
        combine(n, 1, 1, HALF, HALF, None)
        ring_copy(n, 2).start()
        combine(n, 3, 2, 0, HALF, None)
        ring_copy(n, 3).start()

    def relay_part(n):
        ring_copy(n, 0).wait_recv()
        combine(n, 1, 1, 0, HALF, 0)
        ring_copy(n, 4).start()
        ring_copy(n, 1).wait_recv()
        combine(n, 3, 2, HALF, HALF, 1)
        ring_copy(n, 5).start()

    def next_copy(n, device):
        return remote(next_s.at[n], next_hbm.at[:, out_cols(n)], next_send.at[n], next_recv.at[n], device)

    def out_part(n):
        return (out_s.at[n], out_hbm.at[:, out_cols(n)], n)

    def finish_part(n):
        for index in (2, 3, 4, 5):
            ring_copy(n, index).wait_recv()

        def rows_step(step, carry):
            rows = aligned(step * 16, 16)
            total = own_part[n, 2, rows, :] + sib_in[n, 2, rows, :].astype(jnp.float32)
            total = total + arrived[n, 0, rows, :].astype(jnp.float32)
            total = total + arrived[n, 1, rows, :].astype(jnp.float32)
            total = x_ref[rows, out_cols(n)].astype(jnp.float32) + total
            out_s[n, rows, :] = total
            if first:
                next_s[n, rows, :] = total.astype(jnp.bfloat16)
            return carry

        lax.fori_loop(0, ROWS // 16, rows_step, 0)
        if first:
            @pl.when(has_next)
            def _():
                next_copy(n, after).start()

            pltpu.make_async_copy(out_s.at[n], out_hbm.at[:, out_cols(n)], out_recv.at[n]).start()
        else:
            hand_over(*out_part(n), out_send, out_recv)

    if not first:
        load_out.wait()

    def pipeline(i, carry):
        @pl.when(i < PARTS)
        def _():
            project_part(i)

        @pl.when((i >= 1) & (i < PARTS + 1))
        def _():
            send_part(i - 1)

        @pl.when((i >= 2) & (i < PARTS + 2))
        def _():
            relay_part(i - 2)

        @pl.when(i >= 3)
        def _():
            finish_part(i - 3)

        return carry

    lax.fori_loop(0, PARTS + 3, pipeline, 0)

    if first:
        for copy in shares:
            copy.wait_send()
        handed_over(gain_hbm, gain_ref, 0)
        handed_over(wk_hbm, kv_partner[0], 1)
        handed_over(wv_hbm, kv_partner[1], 2)
        keep_gain.wait()
        keep_q.wait()
        keep_kv.wait()

        @pl.when(core == 1)
        def _():
            tree(0, e_acc, sibling).wait_send()

        @pl.when(sends_2)
        def _():
            tree(1, e_acc, (pipe - 2, tensor)).wait_send()

        @pl.when(sends_3)
        def _():
            tree(2, e_acc, (pipe - 4, tensor)).wait_send()

        @pl.when(sends_4)
        def _():
            tree(3, e_acc, (pipe - 8, tensor)).wait_send()

        @pl.when(is_root)
        def _():
            for t in range(8):
                src, dst = spread(t, tensor)

                @pl.when(jnp.logical_not((t % 2 == 0) & (tensor == 2 * (t // 2))))
                def _(src=src, dst=dst, t=t):
                    remote(src, dst, all_send.at[t], all_recv.at[tensor], (t % 2, 2 * (t // 2))).wait_send()

        @pl.when(enters)
        def _():
            for t in range(8):
                src, dst = spread(0, t)
                remote(src, dst, all_send.at[0], all_recv.at[t], sibling).wait_recv()

    else:
        handed(held_src, held_out, 0)
        handed_over(held_src, held_out, 0)

    for copy in sends:
        copy.wait_send()

    def drain(n, carry):
        sib_copy(n).wait_send()
        for index in range(6):
            ring_copy(n, index).wait_send()
        if first:
            @pl.when(has_next)
            def _():
                next_copy(n, after).wait_send()

            @pl.when(has_prev)
            def _():
                next_copy(n, after).wait_recv()

            pltpu.make_async_copy(out_s.at[n], out_hbm.at[:, out_cols(n)], out_recv.at[n]).wait()
            keep_part(n).wait()
        else:
            handed(*out_part(n), out_send, out_recv)
            handed_over(*out_part(n), out_send, out_recv)
        return carry

    lax.fori_loop(0, PARTS, drain, 0)


def layer(first, *operands):
    bf16, f32 = jnp.bfloat16, jnp.float32
    dma = pltpu.SemaphoreType.DMA
    hbm = pl.BlockSpec(memory_space=pl.ANY)
    block = jax.ShapeDtypeStruct((ROWS, WIDTH), f32)
    if first:
        out_shape = (
            block,
            jax.ShapeDtypeStruct((ROWS, WIDTH), bf16),
            jax.ShapeDtypeStruct((1, WIDTH), f32),
            jax.ShapeDtypeStruct((WIDTH, 512), bf16),
            jax.ShapeDtypeStruct((256, WIDTH), bf16),
            jax.ShapeDtypeStruct((512, WIDTH), bf16),
        )
    else:
        out_shape = (block, block)
    scratch = [
        pltpu.VMEM((ROWS, WIDTH), bf16),
        pltpu.VMEM((1, WIDTH), f32),
        pltpu.VMEM((WIDTH, 512), bf16),
        pltpu.VMEM((256, WIDTH), bf16),
        pltpu.VMEM((512, WIDTH), bf16),
        pltpu.VMEM((RING, PAIR, WIDTH), bf16),
        pltpu.VMEM((HEADS_DEV, TOKENS, HEAD_DIM), bf16),
        pltpu.VMEM((TOKENS, HEAD_DIM), bf16),
        pltpu.VMEM((TOKENS, HEAD_DIM), bf16),
        pltpu.VMEM((RING, PAIR, 512), bf16),
        pltpu.VMEM((PARTS, 4, ROWS, PART), f32),
        pltpu.VMEM((PARTS, 4, ROWS, PART), bf16),
        pltpu.VMEM((PARTS, 4, ROWS, PART), bf16),
        pltpu.VMEM((PARTS, 3, ROWS, PART), bf16),
        pltpu.VMEM((PARTS, 2, HALF, PART), bf16),
        pltpu.VMEM((PARTS, 2, ROWS, PART), bf16),
        pltpu.VMEM((PARTS, ROWS, PART), f32),
        dma((5,)), dma((PARTS,)), dma((4,)), dma((14,)), dma((RING, 2, 2)),
        dma((PARTS,)), dma((PARTS,)), dma((PARTS, 6)), dma((PARTS, 6)),
        dma((4 + PARTS,)), dma((4 + PARTS,)), dma((PARTS,)), dma((PARTS,)),
    ]
    if first:
        scratch += [
            pltpu.VMEM((PARTS, ROWS, PART), bf16),
            pltpu.VMEM((TOKENS, COLS), bf16),
            pltpu.VMEM((4, TOKENS, COLS), bf16),
            dma((1,)), dma((4,)), dma((4,)), dma((8,)), dma((8,)), dma((PARTS,)), dma((PARTS,)),
        ]
    return pl.pallas_call(
        functools.partial(layer_kernel, first),
        out_shape=out_shape,
        in_specs=[hbm] * len(operands),
        out_specs=tuple(hbm for _ in out_shape),
        scratch_shapes=scratch,
        compiler_params=pltpu.CompilerParams(
            collective_id=0 if first else 1, has_side_effects=True, vmem_limit_bytes=60 << 20
        ),
        cost_estimate=pl.CostEstimate(flops=12 * 10**9, bytes_accessed=16 << 20, transcendentals=4 << 20),
        name="first_layer" if first else "second_layer",
    )(*operands)


def body(
    entry_symbol_ids,
    lookup_table_matrix,
    pending_batches,
    scale_factors,
    query_projector,
    key_projector,
    value_projector,
    result_projector,
):
    pipe_pos = lax.axis_index("pipe")
    vocab_dev = lookup_table_matrix.shape[0]
    local_index = entry_symbol_ids - pipe_pos * vocab_dev
    inside = (local_index >= 0) & (local_index < vocab_dev)
    looked = jnp.take(lookup_table_matrix, jnp.clip(local_index, 0, vocab_dev - 1), axis=0)
    looked = jnp.where(inside[:, None], looked, jnp.zeros_like(looked))
    first_held, second_in, *weights = layer(
        True, pending_batches, from_partner(pending_batches), scale_factors, query_projector[0],
        key_projector[0].T, value_projector[0].T, result_projector[0], looked,
    )
    return layer(False, second_in, *weights, first_held)


def solution(mesh):
    in_specs = (
        P(),
        P("pipe", "tensor"),
        P(("pipe", "tensor"), None),
        P("pipe", None),
        P("pipe", None, "tensor"),
        P("pipe", None, "tensor"),
        P("pipe", None, "tensor"),
        P("pipe", "tensor", None),
    )
    out_specs = (P(("pipe", "tensor"), None), P(("pipe", "tensor"), None))
    return jax.shard_map(body, mesh=mesh, in_specs=in_specs, out_specs=out_specs, check_vma=False)
```

```python
import functools

import jax
import jax.numpy as jnp
from jax import lax
from jax.experimental import pallas as pl
from jax.experimental.pallas import tpu as pltpu
from jax.sharding import PartitionSpec as P

HEAD_DIM = 128
MESH = pl.DeviceIdType.MESH
BOTH = ("pipe", "tensor")
SECTIONS = 16
RING = 4
TOKENS = 1024
ROWS = 128
WIDTH = 4096
COLS = 512
HEADS_DEV = 4
PAIR = 2 * ROWS
HALF = ROWS // 2
PARTS = 8
PART = WIDTH // PARTS


def flat(pipe, tensor):
    return pipe * 8 + tensor


def physical(section, block):
    return flat(2 * (section // 2) + block % 2, 2 * (block // 2) + section % 2)


def from_partner(array):
    route = [(flat(s, t), physical(s, t)) for s in range(SECTIONS) for t in range(8)]
    return lax.ppermute(array, BOTH, [(a, b) for a, b in route if a != b])


def remote(src, dst, send_sem, recv_sem, device):
    return pltpu.make_async_remote_copy(
        src_ref=src, dst_ref=dst, send_sem=send_sem, recv_sem=recv_sem,
        device_id=device, device_id_type=MESH,
    )


def aligned(start, size):
    return pl.ds(pl.multiple_of(start, size), size)


def layer_kernel(first, *refs):
    if first:
        (x_hbm, x_got_hbm, gain_hbm, wq_hbm, wk_hbm, wv_hbm, wo_hbm, looked_hbm,
         out_hbm, next_hbm, gain_keep, wq_keep, kv_keep, wo_keep, *refs) = refs
    else:
        (x_hbm, gain_hbm, wq_hbm, kv_hbm, wo_hbm, held_hbm, held_out, out_hbm, *refs) = refs
    (x_ref, gain_ref, w_q, w_kv, w_out, normed, q_s, k_s, v_s, ctx, own_part, sib_out, sib_in, ring_out, relay, arrived,
     out_s, load_sem, wo_sem, kv_sem, ag_send, ag_recv, sib_send, sib_recv, ring_send, ring_recv,
     trade_send, trade_recv, out_send, out_recv, *refs) = refs
    if first:
        next_s, e_acc, e_in, e_sem, e_send, e_recv, all_send, all_recv, next_send, next_recv = refs

    pipe = lax.axis_index("pipe")
    tensor = lax.axis_index("tensor")
    core = lax.rem(pipe, 2)
    x_pos = lax.rem(lax.div(pipe, 2), 4)
    z_hi = lax.div(pipe, 8)
    y = lax.div(tensor, 2)
    z_lo = lax.rem(tensor, 2)
    y_up = lax.rem(y + 1, RING)
    y_far = lax.rem(y + 2, RING)
    y_down = lax.rem(y + 3, RING)
    other = 1 - core
    section = pipe - core + z_lo
    sibling = (pipe + 1 - 2 * core, tensor)
    up = (pipe, 2 * y_up + z_lo)
    down = (pipe, 2 * y_down + z_lo)
    stays = core == z_lo
    moves = core != z_lo
    partner = (pipe - core + z_lo, tensor - z_lo + core)
    has_next = section < SECTIONS - 1
    has_prev = section > 0
    after = (pipe + 2 * z_lo, tensor + 1 - 2 * z_lo)
    before = (pipe - 2 * (1 - z_lo), tensor + 1 - 2 * z_lo)

    barrier = pltpu.get_barrier_semaphore()
    greeted = []

    def greet(device, condition=None):
        def signal():
            pl.semaphore_signal(barrier, inc=1, device_id=device, device_id_type=MESH)

        if condition is None:
            signal()
            greeted.append(1)
        else:
            pl.when(condition)(signal)
            greeted.append(jnp.where(condition, 1, 0))

    greet(sibling)
    greet(up)
    greet(down)
    greet(partner, moves)
    if first:
        lead = core == 0
        x_odd = lax.rem(x_pos, 2) == 1
        sends_2 = lead & x_odd
        takes_2 = lead & (lax.rem(x_pos, 2) == 0)
        sends_3 = lead & (x_pos == 2)
        takes_3 = lead & (x_pos == 0)
        sends_4 = lead & (x_pos == 0) & (z_hi == 1)
        is_root = pipe == 0
        enters = (section == 0)
        greet(after, has_next)
        greet(before, has_prev)
        greet((pipe - 2, tensor), sends_2)
        greet((pipe + 2, tensor), takes_2)
        greet((pipe - 4, tensor), sends_3)
        greet((pipe + 4, tensor), takes_3)
        greet((pipe - 8, tensor), sends_4)
        greet((pipe + 8, tensor), is_root)
        for t in range(8):
            is_me = (pipe == t % 2) & (tensor == 2 * (t // 2))
            greet((t % 2, 2 * (t // 2)), is_root & jnp.logical_not(is_me))
            greet((0, t), enters & jnp.logical_not(is_root & (tensor == t)))
        load_looked = pltpu.make_async_copy(looked_hbm, e_acc, e_sem.at[0])
        load_looked.start()

        @pl.when(stays)
        def _():
            pltpu.make_async_copy(x_hbm, x_ref, load_sem.at[0]).start()

        @pl.when(moves)
        def _():
            pltpu.make_async_copy(x_got_hbm, x_ref, load_sem.at[0]).start()

    else:
        load_gain = pltpu.make_async_copy(gain_hbm, gain_ref, load_sem.at[1])
        load_gain.start()
        pltpu.make_async_copy(x_hbm, x_ref, load_sem.at[0]).start()
        load_q = pltpu.make_async_copy(wq_hbm, w_q, load_sem.at[2])
        load_q.start()
        load_kv = pltpu.make_async_copy(kv_hbm, w_kv, load_sem.at[3])
        load_kv.start()
        load_out = pltpu.make_async_copy(wo_hbm, w_out, load_sem.at[4])
        load_out.start()

    pl.semaphore_wait(barrier, functools.reduce(lambda a, b: a + b, greeted))

    def hand_over(src, dst, slot, sends=trade_send, recvs=trade_recv):
        @pl.when(stays)
        def _():
            pltpu.make_async_copy(src, dst, recvs.at[slot]).start()

        @pl.when(moves)
        def _():
            remote(src, dst, sends.at[slot], recvs.at[slot], partner).start()

    def handed(src, dst, slot, sends=trade_send, recvs=trade_recv):
        remote(src, dst, sends.at[slot], recvs.at[slot], partner).wait_recv()

    def handed_over(src, dst, slot, sends=trade_send, recvs=trade_recv):
        @pl.when(moves)
        def _():
            remote(src, dst, sends.at[slot], recvs.at[slot], partner).wait_send()

    def kv_rows(base, block):
        return w_kv.at[aligned(base + block * 64, 64), :]

    if first:
        kv_mine = (kv_rows(0, core), kv_rows(128, core))
        kv_partner = (kv_rows(0, z_lo), kv_rows(128, z_lo))
        kv_rest = (kv_rows(0, other), kv_rows(128, other))
        hand_over(gain_hbm, gain_ref, 0)
        hand_over(wk_hbm, kv_partner[0], 1)
        hand_over(wv_hbm, kv_partner[1], 2)
        hand_over(wq_hbm, w_q, 3)
        handed(gain_hbm, gain_ref, 0)
        keep_gain = pltpu.make_async_copy(gain_ref, gain_keep, load_sem.at[1])
        keep_gain.start()
    else:
        load_gain.wait()
    pltpu.make_async_copy(x_hbm, x_ref, load_sem.at[0]).wait()

    def norm_rows(step, carry):
        x = x_ref[aligned(step * 16, 16), :].astype(jnp.float32)
        scale = lax.rsqrt(jnp.mean(x * x, axis=1, keepdims=True) + 1e-05)
        normed[y, aligned(core * ROWS + step * 16, 16), :] = (x * scale * gain_ref[...]).astype(jnp.bfloat16)
        return carry

    lax.fori_loop(0, ROWS // 16, norm_rows, 0)
    sends = []

    def piece(chip, side, half):
        return normed.at[chip, aligned(side * ROWS + half * HALF, HALF), :]

    def gather(chip, side, half, device):
        part = piece(chip, side, half)
        copy = remote(part, part, ag_send.at[len(sends)], ag_recv.at[chip, side, half], device)
        copy.start()
        sends.append(copy)

    def wait_piece(chip, side, half):
        part = piece(chip, side, half)
        remote(part, part, ag_send.at[0], ag_recv.at[chip, side, half], sibling).wait_recv()

    gather(y, core, 0, up)
    gather(y, core, 1, down)
    gather(y, core, 0, sibling)
    gather(y, core, 1, sibling)
    gather(y, core, 1, up)
    gather(y, core, 0, down)

    def forward_near():
        wait_piece(y_down, core, 0)
        gather(y_down, core, 0, up)
        gather(y_down, core, 0, sibling)
        wait_piece(y_up, core, 1)
        gather(y_up, core, 1, down)
        gather(y_up, core, 1, sibling)
        wait_piece(y_down, core, 1)
        gather(y_down, core, 1, sibling)
        wait_piece(y_up, core, 0)
        gather(y_up, core, 0, sibling)

    def forward_far():
        wait_piece(y_far, core, 0)
        gather(y_far, core, 0, sibling)
        wait_piece(y_far, core, 1)
        gather(y_far, core, 1, sibling)

    def project(chip):
        rows = aligned(chip * PAIR, PAIR)

        def two_heads(n, carry):
            res = jnp.dot(normed[chip], w_q[:, aligned(n * 256, 256)], preferred_element_type=jnp.float32)
            q_s[2 * n, rows, :] = res[:, :128].astype(jnp.bfloat16)
            q_s[2 * n + 1, rows, :] = res[:, 128:].astype(jnp.bfloat16)
            return carry

        lax.fori_loop(0, 2, two_heads, 0)
        res = lax.dot_general(
            normed[chip], w_kv[...], (((1,), (1,)), ((), ())), preferred_element_type=jnp.float32
        )
        k_s[rows, :] = res[:, :128].astype(jnp.bfloat16)
        v_s[rows, :] = res[:, 128:].astype(jnp.bfloat16)

    def out_cols(n):
        return aligned(n * PART, PART)

    if first:
        def wo_part(n):
            return (wo_hbm.at[:, out_cols(n)], w_out.at[:, out_cols(n)], 4 + n)

        def keep_part(n):
            return pltpu.make_async_copy(w_out.at[:, out_cols(n)], wo_keep.at[:, out_cols(n)], wo_sem.at[n])

        for n in range(PARTS):
            hand_over(*wo_part(n))

        def tree(slot, src, device):
            return remote(src, e_in.at[slot], e_send.at[slot], e_recv.at[slot], device)

        def add_in(slot):
            tree(slot, e_acc, sibling).wait_recv()

            def rows_step(step, carry):
                rows = aligned(step * 64, 64)
                e_acc[rows, :] = e_acc[rows, :] + e_in[slot, rows, :]
                return carry

            lax.fori_loop(0, TOKENS // 64, rows_step, 0)

        load_looked.wait()

        @pl.when(core == 1)
        def _():
            tree(0, e_acc, sibling).start()

        @pl.when(lead)
        def _():
            add_in(0)

        @pl.when(sends_2)
        def _():
            tree(1, e_acc, (pipe - 2, tensor)).start()

        forward_near()

        @pl.when(takes_2)
        def _():
            add_in(1)

        @pl.when(sends_3)
        def _():
            tree(2, e_acc, (pipe - 4, tensor)).start()

        forward_far()

        @pl.when(takes_3)
        def _():
            add_in(2)

        @pl.when(sends_4)
        def _():
            tree(3, e_acc, (pipe - 8, tensor)).start()

        shares = []
        for i in range(2):
            handed((wk_hbm, wv_hbm)[i], kv_mine[i], 1 + i)
            shares.append(remote(kv_mine[i], kv_mine[i], kv_sem.at[i], kv_sem.at[2 + i], sibling))
            shares[i].start()
        handed(wq_hbm, w_q, 3)
        for i in range(2):
            remote(kv_rest[i], kv_rest[i], kv_sem.at[i], kv_sem.at[2 + i], sibling).wait_recv()
        keep_q = pltpu.make_async_copy(w_q, wq_keep, load_sem.at[2])
        keep_q.start()
        keep_kv = pltpu.make_async_copy(w_kv, kv_keep, load_sem.at[3])
        keep_kv.start()
        for chip in range(RING):
            for side in range(2):
                @pl.when(core != side)
                def _(chip=chip, side=side):
                    wait_piece(chip, side, 0)
                    wait_piece(chip, side, 1)

        def project_step(chip, carry):
            project(chip)
            return carry

        lax.fori_loop(0, RING, project_step, 0)
    else:
        held_src = held_hbm
        hand_over(held_src, held_out, 0)
        wait_piece(y, other, 0)
        wait_piece(y, other, 1)
        load_q.wait()
        load_kv.wait()
        project(y)
        forward_near()
        for chip in (y_down, y_up):
            wait_piece(chip, other, 0)
            wait_piece(chip, other, 1)
            project(chip)
        forward_far()
        wait_piece(y_far, other, 0)
        wait_piece(y_far, other, 1)
        project(y_far)

    scale = HEAD_DIM ** (-0.5)

    def head(h, carry):
        cols = aligned(h * HEAD_DIM, HEAD_DIM)
        for i in range(RING):
            keys = PAIR * (i + 1)
            scores = lax.dot_general(
                q_s[h, PAIR * i : keys, :], k_s[:keys, :], (((1,), (1,)), ((), ())),
                preferred_element_type=jnp.float32,
            ) * scale
            q_pos = PAIR * i + lax.broadcasted_iota(jnp.int32, (PAIR, keys), 0)
            k_pos = lax.broadcasted_iota(jnp.int32, (PAIR, keys), 1)
            scores = jnp.where(q_pos >= k_pos, scores, -1e30)
            top = jnp.max(scores, axis=1, keepdims=True)
            exps = jnp.exp(scores - top)
            weights = (exps * (1.0 / jnp.sum(exps, axis=1, keepdims=True))).astype(jnp.bfloat16)
            mixed = jnp.dot(weights, v_s[:keys, :], preferred_element_type=jnp.float32)
            ctx[i, :, cols] = mixed.astype(jnp.bfloat16)
        return carry

    lax.fori_loop(0, HEADS_DEV, head, 0)

    if first:
        def spread(t, column):
            return (
                e_acc.at[pl.ds(t * ROWS, ROWS), :],
                next_hbm.at[:, aligned(column * COLS, COLS)],
            )

        @pl.when(is_root)
        def _():
            add_in(3)
            for t in range(8):
                src, dst = spread(t, tensor)
                is_me = (t % 2 == 0) & (tensor == 2 * (t // 2))

                @pl.when(is_me)
                def _(src=src, dst=dst):
                    pltpu.make_async_copy(src, dst, all_recv.at[tensor]).start()

                @pl.when(jnp.logical_not(is_me))
                def _(src=src, dst=dst, t=t):
                    remote(src, dst, all_send.at[t], all_recv.at[tensor], (t % 2, 2 * (t // 2))).start()

    def sib_copy(n):
        return remote(sib_out.at[n], sib_in.at[n], sib_send.at[n], sib_recv.at[n], sibling)

    low, high = pl.ds(0, HALF), pl.ds(HALF, HALF)
    ring_plan = (
        (0, low, "relay", 0, up),
        (0, high, "relay", 1, down),
        (1, high, "arrived", 0, up),
        (2, low, "arrived", 1, down),
        (1, low, "arrived", 0, up),
        (2, high, "arrived", 1, down),
    )

    def ring_copy(n, index):
        slot, rows, into, side, device = ring_plan[index]
        dst = relay.at[n, side] if into == "relay" else arrived.at[n, side, rows]
        return remote(ring_out.at[n, slot, rows], dst, ring_send.at[n, index], ring_recv.at[n, index], device)

    def combine(n, slot, ring_slot, first_row, count, relayed):
        def rows_step(step, carry):
            rows = aligned(first_row + step * 16, 16)
            total = own_part[n, slot, rows, :] + sib_in[n, slot, rows, :].astype(jnp.float32)
            if relayed is not None:
                total = total + relay[n, relayed, aligned(step * 16, 16), :].astype(jnp.float32)
            ring_out[n, ring_slot, rows, :] = total.astype(jnp.bfloat16)
            return carry

        lax.fori_loop(0, count // 16, rows_step, 0)

    def project_part(n):
        if first:
            handed(*wo_part(n))
            keep_part(n).start()

        def slot_step(slot, carry):
            chip = lax.rem(y + 6 - slot, RING)
            res = jnp.dot(ctx[chip], w_out[:, out_cols(n)], preferred_element_type=jnp.float32)
            top, bottom = res[:ROWS], res[ROWS:]
            own_part[n, slot] = jnp.where(core == 0, top, bottom)
            sib_out[n, slot] = jnp.where(core == 0, bottom, top).astype(jnp.bfloat16)
            return carry

        lax.fori_loop(0, 4, slot_step, 0)
        sib_copy(n).start()

    def send_part(n):
        sib_copy(n).wait_recv()
        combine(n, 0, 0, 0, ROWS, None)
        ring_copy(n, 0).start()
        ring_copy(n, 1).start()
        combine(n, 1, 1, HALF, HALF, None)
        ring_copy(n, 2).start()
        combine(n, 3, 2, 0, HALF, None)
        ring_copy(n, 3).start()

    def relay_part(n):
        ring_copy(n, 0).wait_recv()
        combine(n, 1, 1, 0, HALF, 0)
        ring_copy(n, 4).start()
        ring_copy(n, 1).wait_recv()
        combine(n, 3, 2, HALF, HALF, 1)
        ring_copy(n, 5).start()

    def next_copy(n, device):
        return remote(next_s.at[n], next_hbm.at[:, out_cols(n)], next_send.at[n], next_recv.at[n], device)

    def out_part(n):
        return (out_s.at[n], out_hbm.at[:, out_cols(n)], n)

    def finish_part(n):
        for index in (2, 3, 4, 5):
            ring_copy(n, index).wait_recv()

        def rows_step(step, carry):
            rows = aligned(step * 16, 16)
            total = own_part[n, 2, rows, :] + sib_in[n, 2, rows, :].astype(jnp.float32)
            total = total + arrived[n, 0, rows, :].astype(jnp.float32)
            total = total + arrived[n, 1, rows, :].astype(jnp.float32)
            total = x_ref[rows, out_cols(n)].astype(jnp.float32) + total
            out_s[n, rows, :] = total
            if first:
                next_s[n, rows, :] = total.astype(jnp.bfloat16)
            return carry

        lax.fori_loop(0, ROWS // 16, rows_step, 0)
        if first:
            @pl.when(has_next)
            def _():
                next_copy(n, after).start()

            pltpu.make_async_copy(out_s.at[n], out_hbm.at[:, out_cols(n)], out_recv.at[n]).start()
        else:
            hand_over(*out_part(n), out_send, out_recv)

    if not first:
        load_out.wait()

    def pipeline(i, carry):
        @pl.when(i < PARTS)
        def _():
            project_part(i)

        @pl.when((i >= 1) & (i < PARTS + 1))
        def _():
            send_part(i - 1)

        @pl.when((i >= 2) & (i < PARTS + 2))
        def _():
            relay_part(i - 2)

        @pl.when(i >= 3)
        def _():
            finish_part(i - 3)

        return carry

    lax.fori_loop(0, PARTS + 3, pipeline, 0)

    if first:
        for copy in shares:
            copy.wait_send()
        handed_over(gain_hbm, gain_ref, 0)
        handed_over(wk_hbm, kv_partner[0], 1)
        handed_over(wv_hbm, kv_partner[1], 2)
        handed_over(wq_hbm, w_q, 3)
        keep_gain.wait()
        keep_q.wait()
        keep_kv.wait()

        @pl.when(core == 1)
        def _():
            tree(0, e_acc, sibling).wait_send()

        @pl.when(sends_2)
        def _():
            tree(1, e_acc, (pipe - 2, tensor)).wait_send()

        @pl.when(sends_3)
        def _():
            tree(2, e_acc, (pipe - 4, tensor)).wait_send()

        @pl.when(sends_4)
        def _():
            tree(3, e_acc, (pipe - 8, tensor)).wait_send()

        @pl.when(is_root)
        def _():
            for t in range(8):
                src, dst = spread(t, tensor)

                @pl.when(jnp.logical_not((t % 2 == 0) & (tensor == 2 * (t // 2))))
                def _(src=src, dst=dst, t=t):
                    remote(src, dst, all_send.at[t], all_recv.at[tensor], (t % 2, 2 * (t // 2))).wait_send()

        @pl.when(enters)
        def _():
            for t in range(8):
                src, dst = spread(0, t)
                remote(src, dst, all_send.at[0], all_recv.at[t], sibling).wait_recv()

    else:
        handed(held_src, held_out, 0)
        handed_over(held_src, held_out, 0)

    for copy in sends:
        copy.wait_send()

    def drain(n, carry):
        sib_copy(n).wait_send()
        for index in range(6):
            ring_copy(n, index).wait_send()
        if first:
            @pl.when(has_next)
            def _():
                next_copy(n, after).wait_send()

            @pl.when(has_prev)
            def _():
                next_copy(n, after).wait_recv()

            pltpu.make_async_copy(out_s.at[n], out_hbm.at[:, out_cols(n)], out_recv.at[n]).wait()
            keep_part(n).wait()
            handed_over(*wo_part(n))
        else:
            handed(*out_part(n), out_send, out_recv)
            handed_over(*out_part(n), out_send, out_recv)
        return carry

    lax.fori_loop(0, PARTS, drain, 0)


def layer(first, *operands):
    bf16, f32 = jnp.bfloat16, jnp.float32
    dma = pltpu.SemaphoreType.DMA
    hbm = pl.BlockSpec(memory_space=pl.ANY)
    block = jax.ShapeDtypeStruct((ROWS, WIDTH), f32)
    if first:
        out_shape = (
            block,
            jax.ShapeDtypeStruct((ROWS, WIDTH), bf16),
            jax.ShapeDtypeStruct((1, WIDTH), f32),
            jax.ShapeDtypeStruct((WIDTH, 512), bf16),
            jax.ShapeDtypeStruct((256, WIDTH), bf16),
            jax.ShapeDtypeStruct((512, WIDTH), bf16),
        )
    else:
        out_shape = (block, block)
    scratch = [
        pltpu.VMEM((ROWS, WIDTH), bf16),
        pltpu.VMEM((1, WIDTH), f32),
        pltpu.VMEM((WIDTH, 512), bf16),
        pltpu.VMEM((256, WIDTH), bf16),
        pltpu.VMEM((512, WIDTH), bf16),
        pltpu.VMEM((RING, PAIR, WIDTH), bf16),
        pltpu.VMEM((HEADS_DEV, TOKENS, HEAD_DIM), bf16),
        pltpu.VMEM((TOKENS, HEAD_DIM), bf16),
        pltpu.VMEM((TOKENS, HEAD_DIM), bf16),
        pltpu.VMEM((RING, PAIR, 512), bf16),
        pltpu.VMEM((PARTS, 4, ROWS, PART), f32),
        pltpu.VMEM((PARTS, 4, ROWS, PART), bf16),
        pltpu.VMEM((PARTS, 4, ROWS, PART), bf16),
        pltpu.VMEM((PARTS, 3, ROWS, PART), bf16),
        pltpu.VMEM((PARTS, 2, HALF, PART), bf16),
        pltpu.VMEM((PARTS, 2, ROWS, PART), bf16),
        pltpu.VMEM((PARTS, ROWS, PART), f32),
        dma((5,)), dma((PARTS,)), dma((4,)), dma((14,)), dma((RING, 2, 2)),
        dma((PARTS,)), dma((PARTS,)), dma((PARTS, 6)), dma((PARTS, 6)),
        dma((4 + PARTS,)), dma((4 + PARTS,)), dma((PARTS,)), dma((PARTS,)),
    ]
    if first:
        scratch += [
            pltpu.VMEM((PARTS, ROWS, PART), bf16),
            pltpu.VMEM((TOKENS, COLS), bf16),
            pltpu.VMEM((4, TOKENS, COLS), bf16),
            dma((1,)), dma((4,)), dma((4,)), dma((8,)), dma((8,)), dma((PARTS,)), dma((PARTS,)),
        ]
    return pl.pallas_call(
        functools.partial(layer_kernel, first),
        out_shape=out_shape,
        in_specs=[hbm] * len(operands),
        out_specs=tuple(hbm for _ in out_shape),
        scratch_shapes=scratch,
        compiler_params=pltpu.CompilerParams(
            collective_id=0 if first else 1, has_side_effects=True, vmem_limit_bytes=60 << 20
        ),
        cost_estimate=pl.CostEstimate(flops=12 * 10**9, bytes_accessed=16 << 20, transcendentals=4 << 20),
        name="first_layer" if first else "second_layer",
    )(*operands)


def body(
    entry_symbol_ids,
    lookup_table_matrix,
    pending_batches,
    scale_factors,
    query_projector,
    key_projector,
    value_projector,
    result_projector,
):
    pipe_pos = lax.axis_index("pipe")
    vocab_dev = lookup_table_matrix.shape[0]
    local_index = entry_symbol_ids - pipe_pos * vocab_dev
    inside = (local_index >= 0) & (local_index < vocab_dev)
    looked = jnp.take(lookup_table_matrix, jnp.clip(local_index, 0, vocab_dev - 1), axis=0)
    looked = jnp.where(inside[:, None], looked, jnp.zeros_like(looked))
    first_held, second_in, *weights = layer(
        True, pending_batches, from_partner(pending_batches), scale_factors, query_projector[0],
        key_projector[0].T, value_projector[0].T, result_projector[0], looked,
    )
    return layer(False, second_in, *weights, first_held)


def solution(mesh):
    in_specs = (
        P(),
        P("pipe", "tensor"),
        P(("pipe", "tensor"), None),
        P("pipe", None),
        P("pipe", None, "tensor"),
        P("pipe", None, "tensor"),
        P("pipe", None, "tensor"),
        P("pipe", "tensor", None),
    )
    out_specs = (P(("pipe", "tensor"), None), P(("pipe", "tensor"), None))
    return jax.shard_map(body, mesh=mesh, in_specs=in_specs, out_specs=out_specs, check_vma=False)
```

```python
import functools

import jax
import jax.numpy as jnp
from jax import lax
from jax.experimental import pallas as pl
from jax.experimental.pallas import tpu as pltpu
from jax.sharding import PartitionSpec as P

HEAD_DIM = 128
MESH = pl.DeviceIdType.MESH
SECTIONS = 16
RING = 4
TOKENS = 1024
ROWS = 128
WIDTH = 4096
COLS = 512
HEADS_DEV = 4
PAIR = 2 * ROWS
HALF = ROWS // 2
PARTS = 8
PART = WIDTH // PARTS
HELD = 4
VOCAB_DEV = 8192
CHUNK = 1024
CHUNKS = VOCAB_DEV // CHUNK
QUARTER = TOKENS // 4


def remote(src, dst, send_sem, recv_sem, device):
    return pltpu.make_async_remote_copy(
        src_ref=src, dst_ref=dst, send_sem=send_sem, recv_sem=recv_sem,
        device_id=device, device_id_type=MESH,
    )


def aligned(start, size):
    return pl.ds(pl.multiple_of(start, size), size)


def relay_kernel(
    ids_ref, table_hbm, x_hbm, gain_hbm, wq_hbm, wk_hbm, wv_hbm, wo_hbm,
    first_out, second_out,
    x_s, gain_s, w_q, w_kv, w_out, normed, q_s, k_s, v_s, ctx, own_part, sib_out, sib_in, ring_out, relay,
    arrived, out_s, next_s, table_s, e_acc, e_in, e_side, e_sum, e_far,
    table_sem, kv_sem, ag_send, ag_recv, sib_send, sib_recv, ring_send, ring_recv,
    trade_send, trade_recv, out_send, out_recv, next_send, next_recv,
    core_sem, side_send, side_recv, far_sem, all_send, all_recv,
):
    pipe = lax.axis_index("pipe")
    tensor = lax.axis_index("tensor")
    core = lax.rem(pipe, 2)
    x_pos = lax.rem(lax.div(pipe, 2), 4)
    z_hi = lax.div(pipe, 8)
    y = lax.div(tensor, 2)
    z_lo = lax.rem(tensor, 2)
    y_up = lax.rem(y + 1, RING)
    y_far = lax.rem(y + 2, RING)
    y_down = lax.rem(y + 3, RING)
    other = 1 - core
    section = pipe - core + z_lo
    sibling = (pipe + 1 - 2 * core, tensor)
    up = (pipe, 2 * y_up + z_lo)
    down = (pipe, 2 * y_down + z_lo)
    stays = core == z_lo
    moves = core != z_lo
    partner = (pipe - core + z_lo, tensor - z_lo + core)
    has_next = section < SECTIONS - 1
    has_prev = section > 0
    after = (pipe + 2 * z_lo, tensor + 1 - 2 * z_lo)
    before = (pipe - 2 * (1 - z_lo), tensor + 1 - 2 * z_lo)
    lead = core == 0
    lead_near = lead & (z_hi == 0)
    lead_far = lead & (z_hi == 1)
    enters = section == 0

    def side(distance):
        return (z_hi * 8 + 2 * lax.rem(x_pos + distance, 4) + core, tensor)

    def owner(row_block):
        return (row_block, 2 * x_pos)

    def is_owner(row_block):
        return (pipe == row_block) & (tensor == 2 * x_pos)

    barrier = pltpu.get_barrier_semaphore()
    greeted = []

    def greet(device, condition=None):
        def signal():
            pl.semaphore_signal(barrier, inc=1, device_id=device, device_id_type=MESH)

        if condition is None:
            signal()
            greeted.append(1)
        else:
            pl.when(condition)(signal)
            greeted.append(jnp.where(condition, 1, 0))

    greet(sibling)
    greet(up)
    greet(down)
    greet(partner, moves)
    greet(after, has_next)
    greet(before, has_prev)
    for distance in (1, 2, 3):
        greet(side(distance), lead)
    greet((pipe + 8, tensor), lead_near)
    greet((pipe - 8, tensor), lead_far)
    for row_block in range(2):
        greet(owner(row_block), lead_near & jnp.logical_not(is_owner(row_block)))
    for t in range(8):
        greet((2 * y, t), enters & jnp.logical_not((pipe == 2 * y) & (tensor == t)))

    def table_copy(c):
        slot = lax.rem(c, 2)
        return pltpu.make_async_copy(
            table_hbm.at[aligned(c * CHUNK, CHUNK), :], table_s.at[slot], table_sem.at[slot]
        )

    table_copy(0).start()
    table_copy(1).start()
    e_acc[...] = jnp.zeros_like(e_acc)
    pl.semaphore_wait(barrier, functools.reduce(lambda a, b: a + b, greeted))

    def hand_over(src, dst, sends, recvs):
        @pl.when(stays)
        def _():
            pltpu.make_async_copy(src, dst, recvs).start()

        @pl.when(moves)
        def _():
            remote(src, dst, sends, recvs, partner).start()

    def handed(src, dst, sends, recvs):
        remote(src, dst, sends, recvs, partner).wait_recv()

    def handed_over(src, dst, sends, recvs):
        @pl.when(moves)
        def _():
            remote(src, dst, sends, recvs, partner).wait_send()

    def out_cols(n):
        return aligned(n * PART, PART)

    def kv_rows(base, block):
        return w_kv.at[aligned(base + block * 64, 64), :]

    def traded(src, dst, slot):
        return (src, dst, trade_send.at[slot], trade_recv.at[slot])

    kv_mine = (kv_rows(0, core), kv_rows(128, core))
    kv_rest = (kv_rows(0, other), kv_rows(128, other))
    gain_trade = traded(gain_hbm, gain_s, 0)
    x_trade = traded(x_hbm, x_s.at[0], 1)
    kv_trade = (traded(wk_hbm, kv_rows(0, z_lo), 2), traded(wv_hbm, kv_rows(128, z_lo), 3))
    wq_trade = traded(wq_hbm, w_q, 4)

    def wo_trade(n):
        return traded(wo_hbm.at[:, out_cols(n)], w_out.at[:, out_cols(n)], 5 + n)

    for trade in (gain_trade, x_trade, *kv_trade, wq_trade):
        hand_over(*trade)

    def look_up(c, carry):
        table_copy(c).wait()
        start = pipe * VOCAB_DEV + c * CHUNK

        def tile(step, inner):
            rows = aligned(step * 256, 256)
            row_ids = ids_ref[rows, :] - start
            hit = row_ids == lax.broadcasted_iota(jnp.int32, (256, CHUNK), 1)
            ones = jnp.where(hit, 1.0, 0.0).astype(jnp.bfloat16)
            found = jnp.dot(ones, table_s[lax.rem(c, 2)], preferred_element_type=jnp.float32)
            e_acc[rows, :] = e_acc[rows, :] + found.astype(jnp.bfloat16)
            return inner

        lax.fori_loop(0, TOKENS // 256, tile, 0)

        @pl.when(c < CHUNKS - 2)
        def _():
            table_copy(c + 2).start()

        return carry

    def add_rows(into, count, term):
        def rows_step(step, carry):
            rows = aligned(step * 64, 64)
            into[rows, :] = into[rows, :] + term[rows, :]
            return carry

        lax.fori_loop(0, count // 64, rows_step, 0)

    core_copy = remote(e_acc, e_in, core_sem.at[0], core_sem.at[1], sibling)

    def side_copy(distance):
        quarter = aligned(lax.rem(x_pos + distance, 4) * QUARTER, QUARTER)
        return remote(
            e_acc.at[quarter, :], e_side.at[distance - 1],
            side_send.at[distance - 1], side_recv.at[distance - 1], side(distance),
        )

    far_copy = remote(e_sum, e_far, far_sem.at[0], far_sem.at[1], (pipe - 8, tensor))

    def entry_copy(row_block, column):
        return (
            e_sum.at[pl.ds(row_block * ROWS, ROWS), :],
            x_s.at[1, :, aligned(column * COLS, COLS)],
        )

    def next_copy(n):
        return remote(next_s.at[n], x_s.at[1, :, out_cols(n)], next_send.at[n], next_recv.at[n], after)

    low, high = pl.ds(0, HALF), pl.ds(HALF, HALF)
    ring_plan = (
        (0, low, "relay", 0, up),
        (0, high, "relay", 1, down),
        (1, high, "arrived", 0, up),
        (2, low, "arrived", 1, down),
        (1, low, "arrived", 0, up),
        (2, high, "arrived", 1, down),
    )

    def layer(l):
        first = l == 0

        def norm_rows(step, carry):
            x = x_s[l, aligned(step * 16, 16), :].astype(jnp.float32)
            factor = lax.rsqrt(jnp.mean(x * x, axis=1, keepdims=True) + 1e-05)
            normed[y, aligned(core * ROWS + step * 16, 16), :] = (x * factor * gain_s[...]).astype(jnp.bfloat16)
            return carry

        lax.fori_loop(0, ROWS // 16, norm_rows, 0)

        sends = []

        def piece(chip, owner_core, half):
            return normed.at[chip, aligned(owner_core * ROWS + half * HALF, HALF), :]

        def gather(chip, owner_core, half, device):
            part = piece(chip, owner_core, half)
            copy = remote(part, part, ag_send.at[l, len(sends)], ag_recv.at[l, chip, owner_core, half], device)
            copy.start()
            sends.append(copy)

        def wait_piece(chip, owner_core, half):
            part = piece(chip, owner_core, half)
            remote(part, part, ag_send.at[l, 0], ag_recv.at[l, chip, owner_core, half], sibling).wait_recv()

        gather(y, core, 0, up)
        gather(y, core, 1, down)
        gather(y, core, 0, sibling)
        gather(y, core, 1, sibling)
        gather(y, core, 1, up)
        gather(y, core, 0, down)

        def forward_near():
            wait_piece(y_down, core, 0)
            gather(y_down, core, 0, up)
            gather(y_down, core, 0, sibling)
            wait_piece(y_up, core, 1)
            gather(y_up, core, 1, down)
            gather(y_up, core, 1, sibling)
            wait_piece(y_down, core, 1)
            gather(y_down, core, 1, sibling)
            wait_piece(y_up, core, 0)
            gather(y_up, core, 0, sibling)

        def forward_far():
            wait_piece(y_far, core, 0)
            gather(y_far, core, 0, sibling)
            wait_piece(y_far, core, 1)
            gather(y_far, core, 1, sibling)

        def project(chip):
            rows = aligned(chip * PAIR, PAIR)

            def two_heads(n, carry):
                res = jnp.dot(normed[chip], w_q[:, aligned(n * 256, 256)], preferred_element_type=jnp.float32)
                q_s[2 * n, rows, :] = res[:, :128].astype(jnp.bfloat16)
                q_s[2 * n + 1, rows, :] = res[:, 128:].astype(jnp.bfloat16)
                return carry

            lax.fori_loop(0, 2, two_heads, 0)
            res = lax.dot_general(
                normed[chip], w_kv[...], (((1,), (1,)), ((), ())), preferred_element_type=jnp.float32
            )
            k_s[rows, :] = res[:, :128].astype(jnp.bfloat16)
            v_s[rows, :] = res[:, 128:].astype(jnp.bfloat16)

        if first:
            lax.fori_loop(CHUNKS // 2, CHUNKS, look_up, 0)

            @pl.when(core == 1)
            def _():
                core_copy.start()

            forward_near()

            @pl.when(lead)
            def _():
                core_copy.wait_recv()
                add_rows(e_acc, TOKENS, e_in)
                for distance in (1, 2, 3):
                    side_copy(distance).start()

            forward_far()

            @pl.when(lead)
            def _():
                e_sum[...] = e_acc[aligned(x_pos * QUARTER, QUARTER), :]
                for distance in (1, 2, 3):
                    side_copy(distance).wait_recv()
                    add_rows(e_sum, QUARTER, e_side.at[distance - 1])

            @pl.when(lead_far)
            def _():
                far_copy.start()

            for n in range(PARTS):
                hand_over(*wo_trade(n))
            shares = []
            for i in range(2):
                handed(*kv_trade[i][:1], kv_mine[i], *kv_trade[i][2:])
                shares.append(remote(kv_mine[i], kv_mine[i], kv_sem.at[i], kv_sem.at[2 + i], sibling))
                shares[i].start()
            handed(*wq_trade)
            for i in range(2):
                remote(kv_rest[i], kv_rest[i], kv_sem.at[i], kv_sem.at[2 + i], sibling).wait_recv()
            for chip in range(RING):
                for owner_core in range(2):
                    @pl.when(core != owner_core)
                    def _(chip=chip, owner_core=owner_core):
                        wait_piece(chip, owner_core, 0)
                        wait_piece(chip, owner_core, 1)

            def project_step(chip, carry):
                project(chip)
                return carry

            lax.fori_loop(0, RING, project_step, 0)
        else:
            for n in range(PARTS):
                hand_over(*returned(0, n))
            wait_piece(y, other, 0)
            wait_piece(y, other, 1)
            project(y)
            forward_near()
            for chip in (y_down, y_up):
                wait_piece(chip, other, 0)
                wait_piece(chip, other, 1)
                project(chip)
            forward_far()
            wait_piece(y_far, other, 0)
            wait_piece(y_far, other, 1)
            project(y_far)

        scale = HEAD_DIM ** (-0.5)
        seen = lax.broadcasted_iota(jnp.int32, (PAIR, PAIR), 0) >= lax.broadcasted_iota(jnp.int32, (PAIR, PAIR), 1)

        def against(query, keys):
            return lax.dot_general(query, keys, (((1,), (1,)), ((), ())), preferred_element_type=jnp.float32)

        def head(h, carry):
            cols = aligned(h * HEAD_DIM, HEAD_DIM)
            for i in range(RING):
                before_rows, rows = PAIR * i, slice(PAIR * i, PAIR * (i + 1))
                query = q_s[h, rows, :]
                near = jnp.where(seen, against(query, k_s[rows, :]), -1e30)
                top = jnp.max(near, axis=1, keepdims=True)
                if i:
                    past = against(query, k_s[:before_rows, :])
                    top = jnp.maximum(top, jnp.max(past, axis=1, keepdims=True))
                near = jnp.exp((near - top) * scale)
                total = jnp.sum(near, axis=1, keepdims=True)
                if i:
                    past = jnp.exp((past - top) * scale)
                    total = total + jnp.sum(past, axis=1, keepdims=True)
                share = 1.0 / total
                mixed = jnp.dot((near * share).astype(jnp.bfloat16), v_s[rows, :], preferred_element_type=jnp.float32)
                if i:
                    mixed = mixed + jnp.dot(
                        (past * share).astype(jnp.bfloat16), v_s[:before_rows, :], preferred_element_type=jnp.float32
                    )
                ctx[i, :, cols] = mixed.astype(jnp.bfloat16)
            return carry

        lax.fori_loop(0, HEADS_DEV, head, 0)

        if first:
            @pl.when(lead_near)
            def _():
                far_copy.wait_recv()
                add_rows(e_sum, QUARTER, e_far)
                for row_block in range(2):
                    src, dst = entry_copy(row_block, tensor)

                    @pl.when(is_owner(row_block))
                    def _(src=src, dst=dst):
                        pltpu.make_async_copy(src, dst, all_recv.at[tensor]).start()

                    @pl.when(jnp.logical_not(is_owner(row_block)))
                    def _(src=src, dst=dst, row_block=row_block):
                        remote(src, dst, all_send.at[row_block], all_recv.at[tensor], owner(row_block)).start()

        for copy in sends:
            copy.wait_send()
        if first:
            for copy in shares:
                copy.wait_send()

        def sib_copy(n):
            return remote(sib_out.at[n], sib_in.at[n], sib_send.at[l, n], sib_recv.at[l, n], sibling)

        def ring_copy(n, index):
            slot, rows, into, lane, device = ring_plan[index]
            dst = relay.at[n, lane] if into == "relay" else arrived.at[n, lane, rows]
            return remote(
                ring_out.at[n, slot, rows], dst, ring_send.at[l, n, index], ring_recv.at[l, n, index], device
            )

        def combine(n, slot, ring_slot, first_row, count, relayed):
            held = lax.rem(n, HELD)

            def rows_step(step, carry):
                rows = aligned(first_row + step * 16, 16)
                total = own_part[held, slot, rows, :] + sib_in[n, slot, rows, :].astype(jnp.float32)
                if relayed is not None:
                    total = total + relay[n, relayed, aligned(step * 16, 16), :].astype(jnp.float32)
                ring_out[n, ring_slot, rows, :] = total.astype(jnp.bfloat16)
                return carry

            lax.fori_loop(0, count // 16, rows_step, 0)

        def project_part(n):
            if first:
                handed(*wo_trade(n))
            held = lax.rem(n, HELD)

            def slot_step(slot, carry):
                chip = lax.rem(y + 6 - slot, RING)
                res = jnp.dot(ctx[chip], w_out[:, out_cols(n)], preferred_element_type=jnp.float32)
                top, bottom = res[:ROWS], res[ROWS:]
                own_part[held, slot] = jnp.where(core == 0, top, bottom)
                sib_out[n, slot] = jnp.where(core == 0, bottom, top).astype(jnp.bfloat16)
                return carry

            lax.fori_loop(0, 4, slot_step, 0)
            sib_copy(n).start()

        def send_part(n):
            sib_copy(n).wait_recv()
            combine(n, 0, 0, 0, ROWS, None)
            ring_copy(n, 0).start()
            ring_copy(n, 1).start()
            combine(n, 1, 1, HALF, HALF, None)
            ring_copy(n, 2).start()
            combine(n, 3, 2, 0, HALF, None)
            ring_copy(n, 3).start()

        def relay_part(n):
            ring_copy(n, 0).wait_recv()
            combine(n, 1, 1, 0, HALF, 0)
            ring_copy(n, 4).start()
            ring_copy(n, 1).wait_recv()
            combine(n, 3, 2, HALF, HALF, 1)
            ring_copy(n, 5).start()

        def finish_part(n):
            for index in (2, 3, 4, 5):
                ring_copy(n, index).wait_recv()
            held = lax.rem(n, HELD)

            def rows_step(step, carry):
                rows = aligned(step * 16, 16)
                total = own_part[held, 2, rows, :] + sib_in[n, 2, rows, :].astype(jnp.float32)
                total = total + arrived[n, 0, rows, :].astype(jnp.float32)
                total = total + arrived[n, 1, rows, :].astype(jnp.float32)
                total = x_s[l, rows, out_cols(n)].astype(jnp.float32) + total
                out_s[l, n, rows, :] = total
                if first:
                    next_s[n, rows, :] = total.astype(jnp.bfloat16)
                return carry

            lax.fori_loop(0, ROWS // 16, rows_step, 0)
            if first:
                @pl.when(has_next)
                def _():
                    next_copy(n).start()
            else:
                hand_over(*returned(1, n))

        def pipeline(i, carry):
            @pl.when((i >= 1) & (i < PARTS + 1))
            def _():
                send_part(i - 1)

            @pl.when(i < PARTS)
            def _():
                project_part(i)

            @pl.when((i >= 2) & (i < PARTS + 2))
            def _():
                relay_part(i - 2)

            @pl.when(i >= 3)
            def _():
                finish_part(i - 3)

            return carry

        lax.fori_loop(0, PARTS + 3, pipeline, 0)

        def sent(n, carry):
            sib_copy(n).wait_send()
            for index in range(6):
                ring_copy(n, index).wait_send()
            if first:
                handed_over(*wo_trade(n))

                @pl.when(has_next)
                def _():
                    next_copy(n).wait_send()

                @pl.when(has_prev)
                def _():
                    next_copy(n).wait_recv()

            return carry

        lax.fori_loop(0, PARTS, sent, 0)

    def returned(l, n):
        out = (first_out, second_out)[l]
        return (out_s.at[l, n], out.at[:, out_cols(n)], out_send.at[l, n], out_recv.at[l, n])

    lax.fori_loop(0, CHUNKS // 2, look_up, 0)
    handed(*gain_trade)
    handed(*x_trade)
    layer(0)

    @pl.when(enters)
    def _():
        for t in range(8):
            src, dst = entry_copy(0, t)
            remote(src, dst, all_send.at[0], all_recv.at[t], sibling).wait_recv()

    layer(1)

    for trade in (gain_trade, x_trade, *kv_trade, wq_trade):
        handed_over(*trade)

    @pl.when(core == 1)
    def _():
        core_copy.wait_send()

    @pl.when(lead)
    def _():
        for distance in (1, 2, 3):
            side_copy(distance).wait_send()

    @pl.when(lead_far)
    def _():
        far_copy.wait_send()

    @pl.when(lead_near)
    def _():
        for row_block in range(2):
            src, dst = entry_copy(row_block, tensor)

            @pl.when(jnp.logical_not(is_owner(row_block)))
            def _(src=src, dst=dst, row_block=row_block):
                remote(src, dst, all_send.at[row_block], all_recv.at[tensor], owner(row_block)).wait_send()

    def back(n, carry):
        for l in range(2):
            handed(*returned(l, n))
            handed_over(*returned(l, n))
        return carry

    lax.fori_loop(0, PARTS, back, 0)


def relay_layers(ids, *operands):
    bf16, f32 = jnp.bfloat16, jnp.float32
    dma = pltpu.SemaphoreType.DMA
    hbm = pl.BlockSpec(memory_space=pl.ANY)
    block = jax.ShapeDtypeStruct((ROWS, WIDTH), f32)
    return pl.pallas_call(
        relay_kernel,
        out_shape=(block, block),
        in_specs=[pl.BlockSpec(memory_space=pltpu.VMEM)] + [hbm] * len(operands),
        out_specs=(hbm, hbm),
        scratch_shapes=[
            pltpu.VMEM((2, ROWS, WIDTH), bf16),
            pltpu.VMEM((1, WIDTH), f32),
            pltpu.VMEM((WIDTH, 512), bf16),
            pltpu.VMEM((256, WIDTH), bf16),
            pltpu.VMEM((512, WIDTH), bf16),
            pltpu.VMEM((RING, PAIR, WIDTH), bf16),
            pltpu.VMEM((HEADS_DEV, TOKENS, HEAD_DIM), bf16),
            pltpu.VMEM((TOKENS, HEAD_DIM), bf16),
            pltpu.VMEM((TOKENS, HEAD_DIM), bf16),
            pltpu.VMEM((RING, PAIR, 512), bf16),
            pltpu.VMEM((HELD, 4, ROWS, PART), f32),
            pltpu.VMEM((PARTS, 4, ROWS, PART), bf16),
            pltpu.VMEM((PARTS, 4, ROWS, PART), bf16),
            pltpu.VMEM((PARTS, 3, ROWS, PART), bf16),
            pltpu.VMEM((PARTS, 2, HALF, PART), bf16),
            pltpu.VMEM((PARTS, 2, ROWS, PART), bf16),
            pltpu.VMEM((2, PARTS, ROWS, PART), f32),
            pltpu.VMEM((PARTS, ROWS, PART), bf16),
            pltpu.VMEM((2, CHUNK, COLS), bf16),
            pltpu.VMEM((TOKENS, COLS), bf16),
            pltpu.VMEM((TOKENS, COLS), bf16),
            pltpu.VMEM((3, QUARTER, COLS), bf16),
            pltpu.VMEM((QUARTER, COLS), bf16),
            pltpu.VMEM((QUARTER, COLS), bf16),
            dma((2,)), dma((4,)), dma((2, 14)), dma((2, RING, 2, 2)),
            dma((2, PARTS)), dma((2, PARTS)), dma((2, PARTS, 6)), dma((2, PARTS, 6)),
            dma((5 + PARTS,)), dma((5 + PARTS,)), dma((2, PARTS)), dma((2, PARTS)),
            dma((PARTS,)), dma((PARTS,)),
            dma((2,)), dma((3,)), dma((3,)), dma((2,)), dma((2,)), dma((8,)),
        ],
        compiler_params=pltpu.CompilerParams(
            collective_id=0, has_side_effects=True, vmem_limit_bytes=60 << 20
        ),
        cost_estimate=pl.CostEstimate(flops=32 * 10**9, bytes_accessed=32 << 20, transcendentals=8 << 20),
        name="relay_layers",
    )(ids, *operands)


def body(
    entry_symbol_ids,
    lookup_table_matrix,
    pending_batches,
    scale_factors,
    query_projector,
    key_projector,
    value_projector,
    result_projector,
):
    return relay_layers(
        entry_symbol_ids.reshape(TOKENS, 1), lookup_table_matrix, pending_batches, scale_factors,
        query_projector[0], key_projector[0].T, value_projector[0].T, result_projector[0],
    )


def solution(mesh):
    in_specs = (
        P(),
        P("pipe", "tensor"),
        P(("pipe", "tensor"), None),
        P("pipe", None),
        P("pipe", None, "tensor"),
        P("pipe", None, "tensor"),
        P("pipe", None, "tensor"),
        P("pipe", "tensor", None),
    )
    out_specs = (P(("pipe", "tensor"), None), P(("pipe", "tensor"), None))
    return jax.shard_map(body, mesh=mesh, in_specs=in_specs, out_specs=out_specs, check_vma=False)
```
